32 devices in a mesh: parts: 2 (over x), ctx: 16 (over z, y, core).
Axes of the slice: x: 2, y: 2, z: 4, core: 2. Of those that a mesh axis runs over, the one named last changes fastest.
Arguments:
- values: bfloat16 [4096, 2048], P(('parts', 'ctx')), parts along dimension 0, may hold values from -6 to 6
- gating: bfloat16 [4096, 2048], P(('parts', 'ctx')), parts along dimension 0, may hold values from -6 to 6
- out_weight: bfloat16 [4096, 2048], P(('parts', 'ctx')), parts along dimension 0, may hold values from -0.125 to 0.125
- residue: float32 [4096, 64], P('parts'), parts along dimension 0, may hold values from -0.03125 to 0.03125
- decay_rate: float32 [32, 64], P('parts'), parts along dimension 0, may hold values from 0.2 to 400
- skip_gain: float32 [4096], P('parts'), parts along dimension 0, may hold values from 0.5 to 1.5
- cotangent: bfloat16 [4096, 2048], P(('parts', 'ctx')), parts along dimension 0, may hold values from -6 to 6
Outputs:
- output: bfloat16 [4096, 2048], P(('parts', 'ctx')), parts along dimension 0
- value_grad: bfloat16 [4096, 2048], P(('parts', 'ctx')), parts along dimension 0
- gate_grad: bfloat16 [4096, 2048], P(('parts', 'ctx')), parts along dimension 0
- weight_grad: float32 [4096, 2048], P(('parts', 'ctx')), parts along dimension 0
The draws below stay inside these ranges and needn't reach their ends.
There are 2 independent parts, one for each index of `parts`. The reference program is written for one: setup_inputs(seed, part) draws one part's arguments, and reference() takes and returns one part's arrays. A program takes and returns all parts, laid end to end along the dimension named above; each array names one. Nothing has to cross between parts.
All inputs are finite; a program needn't handle non-finite values.
Results may differ from the reference program's by a relative error of at most 0.0049.
Values may be sent and summed in bfloat16 or wider, within the bound.
A program may use at most 192 MiB of HBM per device.

```python
import math
import jax
import jax.numpy as jnp
from jax import lax

D = 2048
GROUPS = 16
MODES = 64
SEQ = 2048


def shard_levels(stream_key, dims, pieces, least, high):
    def one(axis_at, shards_of):
        heights = jax.random.uniform(jax.random.fold_in(jax.random.fold_in(stream_key, 6), axis_at), (shards_of,), jnp.float32, least / len(pieces), high / len(pieces))
        return jnp.repeat(jnp.exp(heights), dims[axis_at] // shards_of).reshape((-1,) + (1,) * (len(dims) - axis_at - 1))

    gain = one(*pieces[0])
    for cut in pieces[1:]:
        gain = gain * one(*cut)
    return gain


def noise(key, extent, spread, reach, pieces=(), kind=jnp.bfloat16):
    values = spread * jax.random.normal(key, extent, jnp.float32)
    if pieces:
        values = values * shard_levels(key, extent, pieces, -0.22, 0.18)
    return jnp.clip(values, -reach, reach).astype(kind)


def setup_inputs(seed: int = 0, part: int = 0) -> dict:
    streams_of = jax.random.split(jax.random.key(seed), 8)
    own_keys = jax.random.split(jax.random.fold_in(streams_of[7], part), 8)
    values = noise(own_keys[0], (SEQ, D), 1.0, 6.0, ((0, 16),))
    gating = noise(own_keys[1], (SEQ, D), 1.0, 6.0, ((0, 16),))
    out_weight = noise(own_keys[2], (D, D), D ** -0.5, 0.125, ((0, 16),))
    residue = noise(own_keys[3], (D, MODES), (20 * SEQ) ** -0.5, 0.03125, (), jnp.float32)
    decay_rate = jnp.clip(jnp.exp(jax.random.uniform(own_keys[4], (GROUPS, MODES), jnp.float32, math.log(0.2), math.log(400.0))), 0.2, 400.0)
    skip_gain = jnp.clip(1.0 + 0.1 * jax.random.normal(own_keys[5], (D,), jnp.float32), 0.5, 1.5)
    cotangent = noise(own_keys[6], (SEQ, D), 1.0, 6.0, ((0, 16),))
    return {"values": values, "gating": gating, "out_weight": out_weight, "residue": residue, "decay_rate": decay_rate, "skip_gain": skip_gain, "cotangent": cotangent}


def tap_table(residue, decay_rate):
    channels = D // GROUPS
    lag_axis = jnp.arange(SEQ).astype(jnp.float32)

    def one_group(pair):
        res_group, rate_group = pair
        powers = jnp.exp(-lag_axis[:, None] * (rate_group[None, :] / SEQ))
        return jnp.dot(powers, res_group.T, precision=lax.Precision.HIGHEST)

    return lax.map(one_group, (residue.reshape(GROUPS, channels, MODES), decay_rate))


def causal_conv(tables, signal):
    channels = D // GROUPS
    grouped = signal.reshape(SEQ, GROUPS, channels).transpose(1, 0, 2)

    def one_group(pair):
        taps, piece = pair
        length = 2 * SEQ
        spectrum = jnp.fft.rfft(taps, n=length, axis=0) * jnp.fft.rfft(piece, n=length, axis=0)
        return jnp.fft.irfft(spectrum, n=length, axis=0)[:SEQ]

    result = lax.map(one_group, (tables, grouped))
    return result.transpose(1, 0, 2).reshape(SEQ, D)


def reference(values, gating, out_weight, residue, decay_rate, skip_gain, cotangent):
    tables = tap_table(residue, decay_rate)
    signal = values.astype(jnp.float32)
    gate_float = gating.astype(jnp.float32)
    conv = causal_conv(tables, signal) + skip_gain[None, :] * signal
    mixed = (gate_float * conv).astype(jnp.bfloat16)
    output = jnp.dot(mixed, out_weight, preferred_element_type=jnp.float32).astype(jnp.bfloat16)
    mixed_grad = jnp.dot(cotangent, out_weight.T, preferred_element_type=jnp.float32)
    gate_grad = (mixed_grad * conv).astype(jnp.bfloat16)
    signal_back = mixed_grad * gate_float
    anti = causal_conv(tables, signal_back[::-1])[::-1] + skip_gain[None, :] * signal_back
    value_grad = anti.astype(jnp.bfloat16)
    weight_grad = jnp.dot(mixed.T, cotangent, preferred_element_type=jnp.float32)
    return (output, value_grad, gate_grad, weight_grad)
```

```python
import functools

import jax
import jax.numpy as jnp
from jax import lax
from jax.experimental import pallas as pl
from jax.experimental.pallas import tpu as pltpu
from jax.sharding import PartitionSpec as P

B = 64
F32 = jnp.float32
BF16 = jnp.bfloat16


def dot(a, b):
    return jnp.dot(a, b, preferred_element_type=F32)


def split(a):
    hi = a.astype(BF16)
    return hi, (a - hi.astype(F32)).astype(BF16)


def dot3(a, b):
    ah, al = a
    bh, bl = split(b)
    return dot(ah, bh) + dot(ah, bl) + dot(al, bh)


def iota(shape, dim):
    return lax.broadcasted_iota(jnp.int32, shape, dim).astype(F32)


def make_taps(row_ref, rest_ref, skip_ref, taps_ref, groups):
    modes = rest_ref.shape[1]
    for g in range(groups):
        lag_pow = jnp.exp(-iota((B, modes), 0) * row_ref[g])
        taps = jnp.dot(
            lag_pow, rest_ref[g], preferred_element_type=F32, precision=lax.Precision.HIGHEST
        )
        first = (lax.broadcasted_iota(jnp.int32, taps.shape, 0) == 0).astype(F32)
        taps_ref[g] = taps + first * skip_ref[g]


def local_part(get, taps_ref, col_ref, inner_ref, ends_ref, pad_ref, g, blocks, back, lanes):
    modes = col_ref.shape[1]
    offs = iota((modes, B), 1)
    powers = jnp.exp(-(offs if back else B - 1.0 - offs) * col_ref[g])
    powers = split(powers)
    zeros = jnp.zeros((8, lanes), F32)
    if back:
        pad_ref[B : B + 8, :] = zeros
    else:
        pad_ref[0:8, :] = zeros

    def body(b, carry):
        x = get(b)
        if x.dtype == BF16:
            ends_ref[g, b] = dot(powers[0], x) + dot(powers[1], x)
        else:
            ends_ref[g, b] = dot3(powers, x)
        xf = x.astype(F32)
        if back:
            pad_ref[0:B, :] = xf
        else:
            pad_ref[8 : B + 8, :] = xf
        acc = [jnp.zeros((8, lanes), F32) for _ in range(B // 8)]
        for low in range(8):
            if low == 0:
                shifted = xf
            elif back:
                shifted = pad_ref[low : B + low, :]
            else:
                shifted = pad_ref[8 - low : B + 8 - low, :]
            for high in range(B // 8):
                k = 8 * high + low
                tap = taps_ref[g, k : k + 1, :]
                for r in range(B // 8 - high):
                    if back:
                        acc[r] = acc[r] + tap * shifted[8 * (r + high) : 8 * (r + high) + 8]
                    else:
                        acc[r + high] = acc[r + high] + tap * shifted[8 * r : 8 * r + 8]
        inner_ref[pl.ds(pl.multiple_of(b * B, B), B), g * lanes : (g + 1) * lanes] = (
            jnp.concatenate(acc, axis=0)
        )
        return carry

    lax.fori_loop(0, blocks, body, 0)


def plane_end(ends_ref, col_ref, g, blocks, back):
    step = jnp.exp(-float(B) * col_ref[g])
    total = ends_ref[g, blocks - 1 if back else 0]
    for i in range(1, blocks):
        total = step * total + ends_ref[g, blocks - 1 - i if back else i]
    return total


def finish(state, put, rest_ref, row_ref, col_ref, inner_ref, ends_ref, g, blocks, back, lanes):
    modes = col_ref.shape[1]
    offs = iota((B, modes), 0)
    lead = split(jnp.exp(-(B - offs if back else offs + 1.0) * row_ref[g]))
    step = jnp.exp(-float(B) * col_ref[g])
    for i in range(blocks):
        b = blocks - 1 - i if back else i
        cross = dot3(lead, state * rest_ref[g])
        put(b, inner_ref[b * B : (b + 1) * B, g * lanes : (g + 1) * lanes] + cross)
        state = step * state + ends_ref[g, b]


def incoming(planes_ref, col_ref, g, outer, here, span, back):
    state = jnp.zeros(planes_ref.shape[2:], F32)
    step = jnp.exp(-float(span) * col_ref[g])
    for i in range(outer - 1):
        e = outer - 1 - i if back else i
        use = e > here if back else e < here
        state = jnp.where(use, step * state + planes_ref[e, g].astype(F32), state)
    return state


def first_kernel(x_ref, row_ref, col_ref, rest_ref, skip_ref,
                 inner_ref, ends_ref, end_ref, taps_ref, pad_ref):
    groups, modes, lanes = rest_ref.shape
    blocks = x_ref.shape[0] // B
    make_taps(row_ref, rest_ref, skip_ref, taps_ref, groups)
    for g in range(groups):
        get = lambda b: x_ref[pl.ds(pl.multiple_of(b * B, B), B), g * lanes : (g + 1) * lanes]
        local_part(get, taps_ref, col_ref, inner_ref, ends_ref, pad_ref, g, blocks, False, lanes)
        end_ref[g] = plane_end(ends_ref, col_ref, g, blocks, False).astype(BF16)


def second_kernel(outer, inner_size, planes_ref, inner_ref, ends_ref, gate_ref,
                  row_ref, col_ref, rest_ref, conv_ref, mixed_ref):
    groups, modes, lanes = rest_ref.shape
    tokens = inner_ref.shape[0]
    blocks = tokens // B
    here = lax.axis_index("ctx") // inner_size
    for g in range(groups):
        def put(b, value):
            rows, cols = slice(b * B, (b + 1) * B), slice(g * lanes, (g + 1) * lanes)
            conv_ref[rows, cols] = value
            mixed_ref[rows, cols] = (gate_ref[rows, cols].astype(F32) * value).astype(BF16)

        state = incoming(planes_ref, col_ref, g, outer, here, tokens, False)
        finish(state, put, rest_ref, row_ref, col_ref, inner_ref, ends_ref, g, blocks, False, lanes)


def third_kernel(grad_ref, gate_ref, conv_ref, taps_ref, col_ref,
                 inner_ref, ends_ref, end_ref, gate_grad_ref, pad_ref):
    groups, _, lanes = taps_ref.shape
    blocks = grad_ref.shape[0] // B
    for g in range(groups):
        cols = slice(g * lanes, (g + 1) * lanes)

        def get(b):
            rows = pl.ds(pl.multiple_of(b * B, B), B)
            grad = grad_ref[rows, cols]
            gate_grad_ref[rows, cols] = (grad * conv_ref[rows, cols]).astype(BF16)
            return grad * gate_ref[rows, cols].astype(F32)

        local_part(get, taps_ref, col_ref, inner_ref, ends_ref, pad_ref, g, blocks, True, lanes)
        end_ref[g] = plane_end(ends_ref, col_ref, g, blocks, True).astype(BF16)


def fourth_kernel(outer, inner_size, planes_ref, inner_ref, ends_ref,
                  row_ref, col_ref, rest_ref, value_grad_ref):
    groups, modes, lanes = rest_ref.shape
    tokens = inner_ref.shape[0]
    blocks = tokens // B
    here = lax.axis_index("ctx") // inner_size
    for g in range(groups):
        def put(b, value):
            value_grad_ref[b * B : (b + 1) * B, g * lanes : (g + 1) * lanes] = value.astype(BF16)

        state = incoming(planes_ref, col_ref, g, outer, here, tokens, True)
        finish(state, put, rest_ref, row_ref, col_ref, inner_ref, ends_ref, g, blocks, True, lanes)


def call(kernel, outs, scratch, *args):
    return pl.pallas_call(
        kernel,
        out_shape=[jax.ShapeDtypeStruct(s, d) for s, d in outs],
        in_specs=[pl.BlockSpec(memory_space=pltpu.VMEM)] * len(args),
        out_specs=[pl.BlockSpec(memory_space=pltpu.VMEM)] * len(outs),
        scratch_shapes=scratch,
        compiler_params=pltpu.CompilerParams(vmem_limit_bytes=40 * 2**20),
    )(*args)


def local_tables(residue, decay_rate, skip_gain, seq_total, outer, inner, mine):
    width, modes = residue.shape
    groups = decay_rate.shape[0]
    lanes = width // (outer * inner)
    per_group = width // groups // lanes
    pick = lambda a: lax.dynamic_index_in_dim(a, mine, 1, keepdims=False)
    rates = jnp.repeat(decay_rate / seq_total, per_group, axis=0).reshape(outer, inner, modes)
    rate = pick(rates)
    rest = pick(residue.reshape(outer, inner, lanes, modes)).transpose(0, 2, 1)
    skip = pick(skip_gain.reshape(outer, inner, lanes))
    return rate[:, None, :], rate[:, :, None], rest, skip[:, None, :]


def per_device(inner, values, gating, out_weight, residue, decay_rate, skip_gain, cotangent):
    tokens, width = values.shape
    ctx = lax.axis_size("ctx")
    outer = ctx // inner
    modes = decay_rate.shape[1]
    lanes = width // ctx
    mine = lax.axis_index("ctx") % inner
    span = tokens * inner
    chans = outer * lanes
    planes = [[z * inner + q for q in range(inner)] for z in range(outer)]
    lines = [[z * inner + q for z in range(outer)] for q in range(inner)]
    row, col, rest, skip = local_tables(
        residue, decay_rate, skip_gain, float(tokens * ctx), outer, inner, mine
    )

    def to_channels(a):
        a = a.reshape(tokens, outer, inner, lanes).transpose(2, 0, 1, 3)
        a = lax.all_to_all(a, "ctx", 0, 0, axis_index_groups=planes, tiled=True)
        return a.reshape(span, chans)

    def to_tokens(a):
        a = a.reshape(inner, tokens, outer, lanes)
        a = lax.all_to_all(a, "ctx", 0, 0, axis_index_groups=planes, tiled=True)
        return a.transpose(1, 2, 0, 3).reshape(tokens, width)

    weight = lax.all_gather(out_weight, "ctx", axis=0, tiled=True, axis_index_groups=lines)
    cot = lax.all_gather(cotangent, "ctx", axis=0, tiled=True, axis_index_groups=planes)
    x = to_channels(values)
    gate = to_channels(gating)
    blocks = span // B
    pad = pltpu.VMEM((B + 8, lanes), F32)
    state = (outer, modes, lanes)
    ends_shape = (outer, blocks, modes, lanes)
    inner_f, ends_f, end_f, taps = call(
        first_kernel,
        [((span, chans), F32), (ends_shape, F32), (state, BF16), ((outer, B, lanes), F32)],
        [pad], x, row, col, rest, skip,
    )
    planes_f = lax.all_gather(end_f, "ctx", axis_index_groups=lines)
    conv, mixed = call(
        functools.partial(second_kernel, outer, inner),
        [((span, chans), F32), ((span, chans), BF16)],
        [], planes_f, inner_f, ends_f, gate, row, col, rest,
    )
    partial = jnp.dot(mixed, weight, preferred_element_type=F32).astype(BF16)
    output = lax.psum_scatter(
        partial, "ctx", scatter_dimension=0, tiled=True, axis_index_groups=planes
    )
    weight_part = lax.dot_general(
        mixed, cot, (((0,), (0,)), ((), ())), preferred_element_type=F32
    ).astype(BF16)
    weight_grad = lax.psum_scatter(
        weight_part, "ctx", scatter_dimension=0, tiled=True, axis_index_groups=lines
    ).astype(F32)
    grad = lax.dot_general(cot, weight, (((1,), (1,)), ((), ())), preferred_element_type=F32)
    inner_b, ends_b, end_b, gate_grad = call(
        third_kernel,
        [((span, chans), F32), (ends_shape, F32), (state, BF16), ((span, chans), BF16)],
        [pad], grad, gate, conv, taps, col,
    )
    planes_b = lax.all_gather(end_b, "ctx", axis_index_groups=lines)
    (value_grad,) = call(
        functools.partial(fourth_kernel, outer, inner),
        [((span, chans), BF16)],
        [], planes_b, inner_b, ends_b, row, col, rest,
    )
    return output, to_tokens(value_grad), to_tokens(gate_grad), weight_grad


def solution(mesh):
    rows = P(("parts", "ctx"), None)
    inner = 4
    return jax.shard_map(
        functools.partial(per_device, inner),
        mesh=mesh,
        in_specs=(rows, rows, rows, P("parts", None), P("parts", None), P("parts"), rows),
        out_specs=(rows,) * 4,
        check_vma=False,
    )
```

```python
import functools

import jax
import jax.numpy as jnp
from jax import lax
from jax.experimental import pallas as pl
from jax.experimental.pallas import tpu as pltpu
from jax.sharding import PartitionSpec as P

B = 64
F32 = jnp.float32
BF16 = jnp.bfloat16


def dot(a, b):
    return jnp.dot(a, b, preferred_element_type=F32)


def split(a):
    hi = a.astype(BF16)
    return hi, (a - hi.astype(F32)).astype(BF16)


def dot3(a, b):
    ah, al = a
    bh, bl = split(b)
    return dot(ah, bh) + dot(ah, bl) + dot(al, bh)


def iota(shape, dim):
    return lax.broadcasted_iota(jnp.int32, shape, dim).astype(F32)


def local_tables(residue, decay_rate, skip_gain, seq_total, outer, inner, mine):
    width, modes = residue.shape
    groups = decay_rate.shape[0]
    lanes = width // (outer * inner)
    per_group = width // groups // lanes
    pick = lambda a: lax.dynamic_index_in_dim(a, mine, 1, keepdims=False)
    rates = jnp.repeat(decay_rate / seq_total, per_group, axis=0).reshape(outer, inner, modes)
    rate = pick(rates)
    rest = pick(residue.reshape(outer, inner, lanes, modes)).transpose(0, 2, 1)
    skip = pick(skip_gain.reshape(outer, inner, lanes))
    return rate[:, None, :], rate[:, :, None], rest, skip[:, None, :]


def make_taps(row_ref, rest_ref, skip_ref, taps_ref, groups):
    modes = rest_ref.shape[1]
    for g in range(groups):
        lag_pow = jnp.exp(-iota((B, modes), 0) * row_ref[g])
        taps = jnp.dot(
            lag_pow, rest_ref[g], preferred_element_type=F32, precision=lax.Precision.HIGHEST
        )
        first = (lax.broadcasted_iota(jnp.int32, taps.shape, 0) == 0).astype(F32)
        taps_ref[g] = taps + first * skip_ref[g]


def local_part(get, taps_ref, col_ref, inner_ref, ends_ref, pad_ref, g, blocks, back, lanes):
    modes = col_ref.shape[1]
    offs = iota((modes, B), 1)
    powers = jnp.exp(-(offs if back else B - 1.0 - offs) * col_ref[g])
    powers = split(powers)
    zeros = jnp.zeros((8, lanes), F32)
    if back:
        pad_ref[B : B + 8, :] = zeros
    else:
        pad_ref[0:8, :] = zeros

    def body(b, carry):
        x = get(b)
        if x.dtype == BF16:
            ends_ref[g, b] = dot(powers[0], x) + dot(powers[1], x)
        else:
            ends_ref[g, b] = dot3(powers, x)
        xf = x.astype(F32)
        if back:
            pad_ref[0:B, :] = xf
        else:
            pad_ref[8 : B + 8, :] = xf
        acc = [jnp.zeros((8, lanes), F32) for _ in range(B // 8)]
        for low in range(8):
            if low == 0:
                shifted = xf
            elif back:
                shifted = pad_ref[low : B + low, :]
            else:
                shifted = pad_ref[8 - low : B + 8 - low, :]
            for high in range(B // 8):
                k = 8 * high + low
                tap = taps_ref[g, k : k + 1, :]
                for r in range(B // 8 - high):
                    if back:
                        acc[r] = acc[r] + tap * shifted[8 * (r + high) : 8 * (r + high) + 8]
                    else:
                        acc[r + high] = acc[r + high] + tap * shifted[8 * r : 8 * r + 8]
        inner_ref[g, pl.ds(pl.multiple_of(b * B, B), B), :] = jnp.concatenate(acc, axis=0)
        return carry

    lax.fori_loop(0, blocks, body, 0)


def plane_end(ends_ref, col_ref, g, blocks, back):
    step = jnp.exp(-float(B) * col_ref[g])
    total = ends_ref[g, blocks - 1 if back else 0]
    for i in range(1, blocks):
        total = step * total + ends_ref[g, blocks - 1 - i if back else i]
    return total


def finish(state, put, rest_ref, row_ref, col_ref, inner_ref, ends_ref, g, blocks, back):
    modes = col_ref.shape[1]
    offs = iota((B, modes), 0)
    lead = split(jnp.exp(-(B - offs if back else offs + 1.0) * row_ref[g]))
    step = jnp.exp(-float(B) * col_ref[g])
    for i in range(blocks):
        b = blocks - 1 - i if back else i
        cross = dot3(lead, state * rest_ref[g])
        put(b, inner_ref[g, b * B : (b + 1) * B, :] + cross)
        state = step * state + ends_ref[g, b]


def incoming(planes_ref, col_ref, g, outer, here, span, back):
    state = jnp.zeros(planes_ref.shape[2:], F32)
    step = jnp.exp(-float(span) * col_ref[g])
    for i in range(outer - 1):
        e = outer - 1 - i if back else i
        use = e > here if back else e < here
        state = jnp.where(use, step * state + planes_ref[e, g].astype(F32), state)
    return state


INNER = 4


def kernel(
    outer, val_ref, gat_ref, w_ref, cot_ref, row_ref, col_ref, rest_ref, skip_ref,
    out_ref, vgrad_ref, ggrad_ref, wgrad_ref,
    stage_v, stage_g, x, gate, cots, wbuf, taps, inner, ends, conv, mixed, grad, pad,
    end_f, end_b, planes_f, planes_b, got_g, got_v, outp, out_send, out_got,
    dwp, sum_got, sum_send, send_sems, recv_sems,
):
    tokens, width = val_ref.shape
    groups, modes, lanes = rest_ref.shape
    span = tokens * INNER
    blocks = span // B
    per = tokens // B
    me = lax.axis_index("ctx")
    here, mine = me // INNER, lax.rem(me, INNER)
    hi, lo = mine // 2, lax.rem(mine, 2)
    peers = (hi * 2 + 1 - lo, (1 - hi) * 2 + lo, (1 - hi) * 2 + 1 - lo)
    core, side, far = peers
    not_first, not_last = here > 0, here < outer - 1

    spots = {}

    def sem(name, index=0, size=1):
        if name not in spots:
            spots[name] = sum(s for _, s in spots.values()), size
        return spots[name][0] + index

    def rdma(src, dst, name, index, size, plane, q, recv=None):
        spot = sem(name, index, size)
        got = spot if recv is None else sem(recv[0], recv[1], recv[2])
        return pltpu.make_async_remote_copy(
            src_ref=src, dst_ref=dst, send_sem=send_sems.at[spot], recv_sem=recv_sems.at[got],
            device_id={"ctx": plane * INNER + q}, device_id_type=pl.DeviceIdType.MESH,
        )

    barrier = pltpu.get_barrier_semaphore()
    for q in peers:
        pl.semaphore_signal(
            barrier, inc=1, device_id={"ctx": here * INNER + q},
            device_id_type=pl.DeviceIdType.MESH,
        )
    for d in range(1, outer):
        plane = lax.rem(here + d, outer)
        pl.semaphore_signal(
            barrier, inc=1, device_id={"ctx": plane * INNER + mine},
            device_id_type=pl.DeviceIdType.MESH,
        )
    pl.semaphore_wait(barrier, INNER - 1 + outer - 1)

    def w_right(slot, src):
        return rdma(src, wbuf.at[slot], "w_right", slot, outer, here + 1, mine,
                    ("w", slot, outer))

    def w_left(slot, src):
        return rdma(src, wbuf.at[slot], "w_left", slot, outer, here - 1, mine,
                    ("w", slot, outer))

    sem("w", 0, outer)
    pl.when(not_last)(lambda: w_right(here, w_ref).start())
    pl.when(not_first)(lambda: w_left(here, w_ref).start())

    def w_step(k):
        def from_left():
            slot = here - k
            w_right(slot, wbuf.at[slot]).wait_recv()
            pl.when(not_last)(lambda: w_right(slot, wbuf.at[slot]).start())

        def from_right():
            slot = here + k
            w_left(slot, wbuf.at[slot]).wait_recv()
            pl.when(not_first)(lambda: w_left(slot, wbuf.at[slot]).start())

        pl.when(here - k >= 0)(from_left)
        pl.when(here + k < outer)(from_right)

    def to_channels(stage, dst, name, src):
        if src is not None:
            for q in range(INNER):
                for z in range(outer):
                    at = (z * INNER + q) * lanes
                    stage[q, z] = src[:, at : at + lanes]
        copies = [
            rdma(stage.at[q], dst.at[:, mine], name, i, 3, here, q) for i, q in enumerate(peers)
        ]
        if src is not None:
            for c in copies:
                c.start()
            dst[:, pl.ds(mine, 1)] = stage[pl.ds(mine, 1)].reshape(outer, 1, tokens, lanes)
        return copies

    val_copies = to_channels(stage_v, x, "values", val_ref)
    gat_copies = to_channels(stage_g, gate, "gating", gat_ref)
    cot_core = rdma(cot_ref, cots.at[mine], "cot", 0, 3, here, core)
    cot_side = rdma(cot_ref, cots.at[mine], "cot", 1, 3, here, side)
    cot_next = rdma(cots.at[side], cots.at[side], "cot", 2, 3, here, core)
    cot_side.start()
    cot_core.start()
    wbuf[pl.ds(here, 1)] = w_ref[...].reshape(1, w_ref.shape[0], width)
    cots[pl.ds(mine, 1)] = cot_ref[...].reshape(1, tokens, width)

    make_taps(row_ref, rest_ref, skip_ref, taps, groups)
    for c in val_copies:
        c.wait_recv()

    def forward_group(g, carry):
        def get(b):
            return x[g, b // per, pl.ds(pl.multiple_of(lax.rem(b, per) * B, B), B), :]

        local_part(get, taps, col_ref, inner, ends, pad, g, blocks, False, lanes)
        end_f[g] = plane_end(ends, col_ref, g, blocks, False).astype(BF16)
        return carry

    lax.fori_loop(0, groups, forward_group, 0)

    def states(end, planes, name, e, upward):
        return rdma(end, planes.at[here], name, e, outer, e, mine, (name + "_got", here, outer))

    def states_got(end, planes, name, e):
        return rdma(end, planes.at[e], name, e, outer, e, mine, (name + "_got", e, outer))

    def each(planes_of, act):
        for e in range(outer):
            pl.when(planes_of(e))(functools.partial(act, e))

    sem("fwd", 0, outer)
    sem("fwd_got", 0, outer)
    sem("bwd", 0, outer)
    sem("bwd_got", 0, outer)
    later = lambda e: here < e
    earlier = lambda e: here > e
    each(later, lambda e: states(end_f, planes_f, "fwd", e, True).start())
    w_step(1)
    for c in gat_copies:
        c.wait_recv()
    each(earlier, lambda e: states_got(end_f, planes_f, "fwd", e).wait_recv())
    for g in range(groups):
        def put(b, value):
            rows = slice((b % per) * B, (b % per + 1) * B)
            conv[g, b * B : (b + 1) * B, :] = value
            m = (gate[g, b // per, rows, :].astype(F32) * value).astype(BF16)
            mixed[b * B : (b + 1) * B, g * lanes : (g + 1) * lanes] = m

        state = incoming(planes_f, col_ref, g, outer, here, span, False)
        finish(state, put, rest_ref, row_ref, col_ref, inner, ends, g, blocks, False)

    cot_side.wait_recv()
    cot_next.start()
    for k in range(2, outer - 1):
        w_step(k)
    cot_core.wait_recv()
    cot_next.wait_recv()


    for g in range(groups):
        dwp[g] = lax.dot_general(
            mixed[:, g * lanes : (g + 1) * lanes], cots[...].reshape(span, width),
            (((0,), (0,)), ((), ())), preferred_element_type=F32,
        )

    def right_copy(e):
        return rdma(sum_send.at[e], sum_got.at[e + 1], "sum_right", e, outer, here + 1, mine)

    def left_copy(e):
        return rdma(sum_send.at[e], sum_got.at[e], "sum_left", e, outer, here - 1, mine)

    def start_right(e):
        sum_send[e] = dwp[e].astype(BF16)
        right_copy(e).start()

    def start_left(e):
        sum_send[e] = dwp[e].astype(BF16)
        left_copy(e).start()

    def pass_right(e):
        right_copy(e).wait_recv()
        sum_send[e] = (dwp[e] + sum_got[e + 1].astype(F32)).astype(BF16)
        right_copy(e).start()

    def pass_left(e):
        left_copy(e).wait_recv()
        sum_send[e] = (dwp[e] + sum_got[e].astype(F32)).astype(BF16)
        left_copy(e).start()

    for k in range(1, outer):
        pl.when(here == 0)(functools.partial(start_right, outer - k))
        pl.when(here == outer - 1)(functools.partial(start_left, k - 1))

    def sum_step(k):
        e = outer - k
        pl.when(jnp.logical_and(not_first, here < e))(functools.partial(pass_right, e))
        f = k - 1
        pl.when(jnp.logical_and(not_last, here > f))(functools.partial(pass_left, f))

    for c in val_copies + gat_copies:
        c.wait_send()

    def backward_group(g):
        grad[...] = lax.dot_general(
            cots[...].reshape(span, width), wbuf[g], (((1,), (1,)), ((), ())),
            preferred_element_type=F32,
        )

        def get(b):
            rows = pl.ds(pl.multiple_of(b * B, B), B)
            sub = pl.ds(pl.multiple_of(lax.rem(b, per) * B, B), B)
            part = grad[rows, :]
            stage_g[b // per, g, sub, :] = (part * conv[g, rows, :]).astype(BF16)
            return part * gate[g, b // per, sub, :].astype(F32)

        local_part(get, taps, col_ref, inner, ends, pad, g, blocks, True, lanes)
        end_b[g] = plane_end(ends, col_ref, g, blocks, True).astype(BF16)

    backward_group(here)

    def around(k, carry):
        pl.when(k == outer - 1)(lambda: w_step(outer - 1))
        pl.when(here - k >= 0)(lambda: backward_group(here - k))
        pl.when(here + k < outer)(lambda: backward_group(here + k))
        return carry

    lax.fori_loop(1, outer, around, 0)
    each(earlier, lambda e: states(end_b, planes_b, "bwd", e, False).start())

    def to_tokens(buf, got, name):
        return [
            rdma(buf.at[q], got.at[mine], name, i, 3, here, q) for i, q in enumerate(peers)
        ]

    gg_copies = to_tokens(stage_g, got_g, "gate_grad")
    vg_copies = to_tokens(stage_v, got_v, "value_grad")
    for c in gg_copies:
        c.start()

    weight_rows = groups * w_ref.shape[0]
    chunk = min(512, width)

    def out_term(j, carry):
        cols = pl.ds(pl.multiple_of(j * chunk, chunk), chunk)
        part = dot(mixed[...], wbuf[:, :, cols].reshape(weight_rows, chunk))
        outp[:, :, cols] = part.reshape(INNER, tokens, chunk)
        return carry

    lax.fori_loop(0, width // chunk, out_term, 0)
    out_far = rdma(out_send.at[0], out_got.at[0], "out", 0, 3, here, core)
    out_core = rdma(out_send.at[1], out_got.at[1], "out", 1, 3, here, core)
    out_side = rdma(out_send.at[2], out_got.at[2], "out", 2, 3, here, side)
    out_send[0] = outp[far].astype(BF16)
    out_far.start()
    out_send[1] = outp[core].astype(BF16)
    out_core.start()
    out_far.wait_recv()
    out_send[2] = (outp[side] + out_got[0].astype(F32)).astype(BF16)
    out_side.start()

    each(later, lambda e: states_got(end_b, planes_b, "bwd", e).wait_recv())
    for g in range(groups):
        def put(b, value):
            rows = slice((b % per) * B, (b % per + 1) * B)
            stage_v[b // per, g, rows, :] = value.astype(BF16)

        state = incoming(planes_b, col_ref, g, outer, here, span, True)
        finish(state, put, rest_ref, row_ref, col_ref, inner, ends, g, blocks, True)
    for c in vg_copies:
        c.start()
    for k in range(1, outer):
        sum_step(k)

    def collect(buf, got, copies, dst):
        got[pl.ds(mine, 1)] = buf[pl.ds(mine, 1)]
        for c in copies:
            c.wait_recv()
        for q in range(INNER):
            for z in range(outer):
                at = (z * INNER + q) * lanes
                dst[:, at : at + lanes] = got[q, z]

    collect(stage_g, got_g, gg_copies, ggrad_ref)
    out_core.wait_recv()
    out_side.wait_recv()
    out_ref[...] = (
        outp[mine] + out_got[1].astype(F32) + out_got[2].astype(F32)
    ).astype(BF16)
    collect(stage_v, got_v, vg_copies, vgrad_ref)

    wgrad_ref[...] = dwp[here]

    def last_right():
        right_copy(here).wait_recv()
        wgrad_ref[...] += sum_got[here + 1].astype(F32)

    def last_left():
        left_copy(here).wait_recv()
        wgrad_ref[...] += sum_got[here].astype(F32)

    pl.when(not_first)(last_right)
    pl.when(not_last)(last_left)

    for c in gg_copies + vg_copies:
        c.wait_send()
    for c in (cot_core, cot_side, cot_next, out_far, out_core, out_side):
        c.wait_send()
    each(later, lambda e: states(end_f, planes_f, "fwd", e, True).wait_send())
    each(earlier, lambda e: states(end_b, planes_b, "bwd", e, False).wait_send())
    for e in range(outer):
        pl.when(jnp.logical_and(not_last, here >= e))(
            lambda e=e: w_right(e, wbuf.at[e]).wait_send()
        )
        pl.when(jnp.logical_and(not_first, here <= e))(
            lambda e=e: w_left(e, wbuf.at[e]).wait_send()
        )
        pl.when(here < e)(lambda e=e: right_copy(e).wait_send())
        pl.when(here > e)(lambda e=e: left_copy(e).wait_send())
    assert sum(s for _, s in spots.values()) <= send_sems.shape[0]


def per_device(values, gating, out_weight, residue, decay_rate, skip_gain, cotangent):
    tokens, width = values.shape
    ctx = lax.axis_size("ctx")
    outer = ctx // INNER
    modes = decay_rate.shape[1]
    lanes = width // ctx
    rows = out_weight.shape[0]
    span = tokens * INNER
    mine = lax.axis_index("ctx") % INNER
    row, col, rest, skip = local_tables(
        residue, decay_rate, skip_gain, float(tokens * ctx), outer, INNER, mine
    )
    quarter = (INNER, outer, tokens, lanes)
    chans = (outer, INNER, tokens, lanes)
    state = (outer, modes, lanes)
    slots = (outer, rows, width)
    scratch = [
        (quarter, BF16), (quarter, BF16), (chans, BF16), (chans, BF16),
        ((INNER, tokens, width), BF16), (slots, BF16), ((outer, B, lanes), F32),
        ((outer, span, lanes), F32), ((outer, span // B, modes, lanes), F32),
        ((outer, span, lanes), F32), ((span, outer * lanes), BF16), ((span, lanes), F32), ((B + 8, lanes), F32),
        (state, BF16), (state, BF16), ((outer,) + state, BF16), ((outer,) + state, BF16),
        (quarter, BF16), (quarter, BF16),
        ((INNER, tokens, width), F32), ((3, tokens, width), BF16), ((3, tokens, width), BF16),
        (slots, F32), ((outer + 1, rows, width), BF16), (slots, BF16),
    ]
    sems = pltpu.SemaphoreType.DMA((18 + 9 * outer,))
    args = (values, gating, out_weight, cotangent, row, col, rest, skip)
    out = jax.ShapeDtypeStruct((tokens, width), BF16)
    macs = 3 * span * outer * lanes * width
    return pl.pallas_call(
        functools.partial(kernel, outer),
        out_shape=[out, out, out, jax.ShapeDtypeStruct((rows, width), F32)],
        in_specs=[pl.BlockSpec(memory_space=pltpu.VMEM)] * len(args),
        out_specs=[pl.BlockSpec(memory_space=pltpu.VMEM)] * 4,
        scratch_shapes=[pltpu.VMEM(s, d) for s, d in scratch] + [sems, sems],
        compiler_params=pltpu.CompilerParams(
            collective_id=0, has_side_effects=True, vmem_limit_bytes=61 * 2**20
        ),
        cost_estimate=pl.CostEstimate(
            flops=2 * macs, bytes_accessed=6 * 2**20, transcendentals=0
        ),
    )(*args)


def solution(mesh):
    rows = P(("parts", "ctx"), None)
    return jax.shard_map(
        per_device,
        mesh=mesh,
        in_specs=(rows, rows, rows, P("parts", None), P("parts", None), P("parts"), rows),
        out_specs=(rows,) * 4,
        check_vma=False,
    )
```

```python
import functools

import jax
import jax.numpy as jnp
from jax import lax
from jax.experimental import pallas as pl
from jax.experimental.pallas import tpu as pltpu
from jax.sharding import PartitionSpec as P

B = 64
F32 = jnp.float32
BF16 = jnp.bfloat16


def dot(a, b):
    return jnp.dot(a, b, preferred_element_type=F32)


def split(a):
    hi = a.astype(BF16)
    return hi, (a - hi.astype(F32)).astype(BF16)


def dot3(a, b):
    ah, al = a
    bh, bl = split(b)
    return dot(ah, bh) + dot(ah, bl) + dot(al, bh)


def iota(shape, dim):
    return lax.broadcasted_iota(jnp.int32, shape, dim).astype(F32)


def make_tables(
    res_ref, rate_ref, skip_ref, row_ref, col_ref, rest_ref, taps_ref, seq_total, outer, mine
):
    _, modes, lanes = rest_ref.shape
    for g in range(outer):
        block = g * INNER + mine
        group = block * rate_ref.shape[0] // (outer * INNER)
        row_ref[g] = rate_ref[pl.ds(group, 1), :] / seq_total
        col_ref[g] = jnp.broadcast_to(row_ref[g], (128, modes)).T
        rest_ref[g] = res_ref[pl.ds(pl.multiple_of(block * lanes, lanes), lanes), :].T
        lag_pow = jnp.exp(-iota((B, modes), 0) * row_ref[g])
        taps = jnp.dot(
            lag_pow, rest_ref[g], preferred_element_type=F32, precision=lax.Precision.HIGHEST
        )
        first = (lax.broadcasted_iota(jnp.int32, taps.shape, 0) == 0).astype(F32)
        taps_ref[g] = taps + first * skip_ref[pl.ds(block, 1), :]


def local_part(get, taps_ref, col_ref, inner_ref, ends_ref, pad_ref, g, blocks, back, lanes):
    modes = col_ref.shape[1]
    offs = iota((modes, B), 1)
    powers = jnp.exp(-(offs if back else B - 1.0 - offs) * col_ref[g][:, :B])
    powers = split(powers)
    zeros = jnp.zeros((8, lanes), F32)
    if back:
        pad_ref[B : B + 8, :] = zeros
    else:
        pad_ref[0:8, :] = zeros

    def body(b, carry):
        x = get(b)
        if x.dtype == BF16:
            ends_ref[g, b] = dot(powers[0], x) + dot(powers[1], x)
        else:
            ends_ref[g, b] = dot3(powers, x)
        xf = x.astype(F32)
        if back:
            pad_ref[0:B, :] = xf
        else:
            pad_ref[8 : B + 8, :] = xf
        acc = [jnp.zeros((8, lanes), F32) for _ in range(B // 8)]
        for low in range(8):
            if low == 0:
                shifted = xf
            elif back:
                shifted = pad_ref[low : B + low, :]
            else:
                shifted = pad_ref[8 - low : B + 8 - low, :]
            for high in range(B // 8):
                k = 8 * high + low
                tap = taps_ref[g, k : k + 1, :]
                for r in range(B // 8 - high):
                    if back:
                        acc[r] = acc[r] + tap * shifted[8 * (r + high) : 8 * (r + high) + 8]
                    else:
                        acc[r + high] = acc[r + high] + tap * shifted[8 * r : 8 * r + 8]
        inner_ref[g, pl.ds(pl.multiple_of(b * B, B), B), :] = jnp.concatenate(acc, axis=0)
        return carry

    lax.fori_loop(0, blocks, body, 0)


def plane_end(ends_ref, col_ref, g, blocks, back):
    total = ends_ref[g, blocks - 1 if back else 0]
    step = jnp.exp(-float(B) * col_ref[g][:, : total.shape[1]])
    for i in range(1, blocks):
        total = step * total + ends_ref[g, blocks - 1 - i if back else i]
    return total


def finish(state, put, rest_ref, row_ref, col_ref, inner_ref, ends_ref, g, blocks, back):
    modes = col_ref.shape[1]
    offs = iota((B, modes), 0)
    lead = split(jnp.exp(-(B - offs if back else offs + 1.0) * row_ref[g]))
    step = jnp.exp(-float(B) * col_ref[g][:, : state.shape[1]])
    for i in range(blocks):
        b = blocks - 1 - i if back else i
        cross = dot3(lead, state * rest_ref[g])
        put(b, inner_ref[g, b * B : (b + 1) * B, :] + cross)
        state = step * state + ends_ref[g, b]


def incoming(planes_ref, col_ref, g, outer, here, span, back):
    state = jnp.zeros(planes_ref.shape[2:], F32)
    step = jnp.exp(-float(span) * col_ref[g][:, : state.shape[1]])
    for i in range(outer - 1):
        e = outer - 1 - i if back else i
        use = e > here if back else e < here
        state = jnp.where(use, step * state + planes_ref[e, g].astype(F32), state)
    return state


INNER = 4


def kernel(
    outer, val_ref, gat_ref, w_ref, cot_ref, res_ref, rate_ref, skip_ref,
    out_ref, vgrad_ref, ggrad_ref, wgrad_ref,
    row_ref, col_ref, rest_ref, stage_v, stage_g, x, gate, cots, wbuf, taps, inner, ends, conv, mixed, grad, pad,
    end_f, end_b, planes_f, planes_b, got_g, got_v, outp, out_send, out_got,
    dwp, sum_got, sum_send, send_sems, recv_sems,
):
    tokens, width = val_ref.shape
    groups, modes, lanes = rest_ref.shape
    span = tokens * INNER
    blocks = span // B
    per = tokens // B
    me = lax.axis_index("ctx")
    here, mine = me // INNER, lax.rem(me, INNER)
    hi, lo = mine // 2, lax.rem(mine, 2)
    peers = (hi * 2 + 1 - lo, (1 - hi) * 2 + lo, (1 - hi) * 2 + 1 - lo)
    core, side, far = peers
    not_first, not_last = here > 0, here < outer - 1

    spots = {}

    def sem(name, index=0, size=1):
        if name not in spots:
            spots[name] = sum(s for _, s in spots.values()), size
        return spots[name][0] + index

    def rdma(src, dst, name, index, size, plane, q, recv=None):
        spot = sem(name, index, size)
        got = spot if recv is None else sem(recv[0], recv[1], recv[2])
        return pltpu.make_async_remote_copy(
            src_ref=src, dst_ref=dst, send_sem=send_sems.at[spot], recv_sem=recv_sems.at[got],
            device_id={"ctx": plane * INNER + q}, device_id_type=pl.DeviceIdType.MESH,
        )

    barrier = pltpu.get_barrier_semaphore()
    for q in peers:
        pl.semaphore_signal(
            barrier, inc=1, device_id={"ctx": here * INNER + q},
            device_id_type=pl.DeviceIdType.MESH,
        )
    for d in range(1, outer):
        plane = lax.rem(here + d, outer)
        pl.semaphore_signal(
            barrier, inc=1, device_id={"ctx": plane * INNER + mine},
            device_id_type=pl.DeviceIdType.MESH,
        )
    pl.semaphore_wait(barrier, INNER - 1 + outer - 1)

    def w_right(slot, src):
        return rdma(src, wbuf.at[slot], "w_right", slot, outer, here + 1, mine,
                    ("w", slot, outer))

    def w_left(slot, src):
        return rdma(src, wbuf.at[slot], "w_left", slot, outer, here - 1, mine,
                    ("w", slot, outer))

    sem("w", 0, outer)
    pl.when(not_last)(lambda: w_right(here, w_ref).start())
    pl.when(not_first)(lambda: w_left(here, w_ref).start())

    def w_step(k):
        def from_left():
            slot = here - k
            w_right(slot, wbuf.at[slot]).wait_recv()
            pl.when(not_last)(lambda: w_right(slot, wbuf.at[slot]).start())

        def from_right():
            slot = here + k
            w_left(slot, wbuf.at[slot]).wait_recv()
            pl.when(not_first)(lambda: w_left(slot, wbuf.at[slot]).start())

        pl.when(here - k >= 0)(from_left)
        pl.when(here + k < outer)(from_right)

    def to_channels(stage, dst, name, src):
        if src is not None:
            for q in range(INNER):
                for z in range(outer):
                    at = (z * INNER + q) * lanes
                    stage[q, z] = src[:, at : at + lanes]
        copies = [
            rdma(stage.at[q], dst.at[:, mine], name, i, 3, here, q) for i, q in enumerate(peers)
        ]
        if src is not None:
            for c in copies:
                c.start()
            dst[:, pl.ds(mine, 1)] = stage[pl.ds(mine, 1)].reshape(outer, 1, tokens, lanes)
        return copies

    val_copies = to_channels(stage_v, x, "values", val_ref)
    cot_core = rdma(cot_ref, cots.at[mine], "cot", 0, 3, here, core)
    cot_side = rdma(cot_ref, cots.at[mine], "cot", 1, 3, here, side)
    cot_next = rdma(cots.at[side], cots.at[side], "cot", 2, 3, here, core)
    cot_core.start()
    make_tables(
        res_ref, rate_ref, skip_ref, row_ref, col_ref, rest_ref, taps,
        float(tokens * outer * INNER), outer, mine,
    )
    gat_copies = to_channels(stage_g, gate, "gating", gat_ref)
    wbuf[pl.ds(here, 1)] = w_ref[...].reshape(1, w_ref.shape[0], width)
    cots[pl.ds(mine, 1)] = cot_ref[...].reshape(1, tokens, width)

    for c in val_copies:
        c.wait_recv()
    cot_side.start()

    def forward_group(g, carry):
        def get(b):
            return x[g, b // per, pl.ds(pl.multiple_of(lax.rem(b, per) * B, B), B), :]

        local_part(get, taps, col_ref, inner, ends, pad, g, blocks, False, lanes)
        end_f[g] = plane_end(ends, col_ref, g, blocks, False).astype(BF16)
        return carry

    lax.fori_loop(0, groups, forward_group, 0)

    def states(end, planes, name, e, upward):
        return rdma(end, planes.at[here], name, e, outer, e, mine, (name + "_got", here, outer))

    def states_got(end, planes, name, e):
        return rdma(end, planes.at[e], name, e, outer, e, mine, (name + "_got", e, outer))

    def each(planes_of, act):
        for e in range(outer):
            pl.when(planes_of(e))(functools.partial(act, e))

    sem("fwd", 0, outer)
    sem("fwd_got", 0, outer)
    sem("bwd", 0, outer)
    sem("bwd_got", 0, outer)
    later = lambda e: here < e
    earlier = lambda e: here > e
    each(later, lambda e: states(end_f, planes_f, "fwd", e, True).start())
    w_step(1)
    for c in gat_copies:
        c.wait_recv()
    each(earlier, lambda e: states_got(end_f, planes_f, "fwd", e).wait_recv())
    for g in range(groups):
        def put(b, value):
            rows = slice((b % per) * B, (b % per + 1) * B)
            conv[g, b * B : (b + 1) * B, :] = value
            m = (gate[g, b // per, rows, :].astype(F32) * value).astype(BF16)
            mixed[b * B : (b + 1) * B, g * lanes : (g + 1) * lanes] = m

        state = incoming(planes_f, col_ref, g, outer, here, span, False)
        finish(state, put, rest_ref, row_ref, col_ref, inner, ends, g, blocks, False)

    cot_side.wait_recv()
    cot_next.start()
    for k in range(2, outer - 1):
        w_step(k)
    cot_core.wait_recv()
    cot_next.wait_recv()


    def right_copy(e):
        return rdma(sum_send.at[e], sum_got.at[e + 1], "sum_right", e, outer, here + 1, mine)

    def left_copy(e):
        return rdma(sum_send.at[e], sum_got.at[e], "sum_left", e, outer, here - 1, mine)

    def start_right(e):
        sum_send[e] = dwp[e].astype(BF16)
        right_copy(e).start()

    def start_left(e):
        sum_send[e] = dwp[e].astype(BF16)
        left_copy(e).start()

    def pass_right(e):
        right_copy(e).wait_recv()
        sum_send[e] = (dwp[e] + sum_got[e + 1].astype(F32)).astype(BF16)
        right_copy(e).start()

    def pass_left(e):
        left_copy(e).wait_recv()
        sum_send[e] = (dwp[e] + sum_got[e].astype(F32)).astype(BF16)
        left_copy(e).start()

    def weight_terms(order, end, start):
        for g in order:
            dwp[g] = lax.dot_general(
                mixed[:, g * lanes : (g + 1) * lanes], cots[...].reshape(span, width),
                (((0,), (0,)), ((), ())), preferred_element_type=F32,
            )
            if g != end:
                pl.when(here == end)(functools.partial(start, g))

    lower = here < outer // 2
    upper = here >= outer // 2
    pl.when(lower)(lambda: weight_terms(range(outer)[::-1], 0, start_right))
    pl.when(upper)(lambda: weight_terms(range(outer), outer - 1, start_left))

    def sum_step(k, near):
        e, f = outer - k, k - 1
        right = jnp.logical_and(not_first, here < e)
        left = jnp.logical_and(not_last, here > f)
        pl.when(jnp.logical_and(lower if near else upper, right))(functools.partial(pass_right, e))
        pl.when(jnp.logical_and(upper if near else lower, left))(functools.partial(pass_left, f))

    for c in val_copies + gat_copies:
        c.wait_send()

    def backward_group(g):
        grad[...] = lax.dot_general(
            cots[...].reshape(span, width), wbuf[g], (((1,), (1,)), ((), ())),
            preferred_element_type=F32,
        )

        def get(b):
            rows = pl.ds(pl.multiple_of(b * B, B), B)
            sub = pl.ds(pl.multiple_of(lax.rem(b, per) * B, B), B)
            part = grad[rows, :]
            stage_g[b // per, g, sub, :] = (part * conv[g, rows, :]).astype(BF16)
            return part * gate[g, b // per, sub, :].astype(F32)

        local_part(get, taps, col_ref, inner, ends, pad, g, blocks, True, lanes)
        end_b[g] = plane_end(ends, col_ref, g, blocks, True).astype(BF16)

    backward_group(here)

    def around(k, carry):
        pl.when(k == outer - 1)(lambda: w_step(outer - 1))
        pl.when(here - k >= 0)(lambda: backward_group(here - k))
        pl.when(here + k < outer)(lambda: backward_group(here + k))
        return carry

    lax.fori_loop(1, outer, around, 0)
    each(earlier, lambda e: states(end_b, planes_b, "bwd", e, False).start())

    def to_tokens(buf, got, name):
        return [
            rdma(buf.at[q], got.at[mine], name, i, 3, here, q) for i, q in enumerate(peers)
        ]

    gg_copies = to_tokens(stage_g, got_g, "gate_grad")
    vg_copies = to_tokens(stage_v, got_v, "value_grad")
    for c in gg_copies:
        c.start()
    sum_step(1, True)

    weight_rows = groups * w_ref.shape[0]
    chunk = min(512, width)

    def out_term(j, carry):
        cols = pl.ds(pl.multiple_of(j * chunk, chunk), chunk)
        part = dot(mixed[...], wbuf[:, :, cols].reshape(weight_rows, chunk))
        outp[:, :, cols] = part.reshape(INNER, tokens, chunk)
        return carry

    lax.fori_loop(0, width // chunk, out_term, 0)
    out_far = rdma(out_send.at[0], out_got.at[0], "out", 0, 3, here, core)
    out_core = rdma(out_send.at[1], out_got.at[1], "out", 1, 3, here, core)
    out_side = rdma(out_send.at[2], out_got.at[2], "out", 2, 3, here, side)
    out_send[0] = outp[far].astype(BF16)
    out_far.start()
    out_send[1] = outp[core].astype(BF16)
    out_core.start()
    out_far.wait_recv()
    out_send[2] = (outp[side] + out_got[0].astype(F32)).astype(BF16)
    out_side.start()

    each(later, lambda e: states_got(end_b, planes_b, "bwd", e).wait_recv())
    for g in range(groups):
        def put(b, value):
            rows = slice((b % per) * B, (b % per + 1) * B)
            stage_v[b // per, g, rows, :] = value.astype(BF16)

        state = incoming(planes_b, col_ref, g, outer, here, span, True)
        finish(state, put, rest_ref, row_ref, col_ref, inner, ends, g, blocks, True)
    for c in vg_copies:
        c.start()
    for k in range(2, outer):
        sum_step(k, True)
    for k in range(1, outer):
        sum_step(k, False)

    def collect(buf, got, copies, dst):
        got[pl.ds(mine, 1)] = buf[pl.ds(mine, 1)]
        for c in copies:
            c.wait_recv()
        for q in range(INNER):
            for z in range(outer):
                at = (z * INNER + q) * lanes
                dst[:, at : at + lanes] = got[q, z]

    collect(stage_g, got_g, gg_copies, ggrad_ref)
    out_core.wait_recv()
    out_side.wait_recv()
    out_ref[...] = (
        outp[mine] + out_got[1].astype(F32) + out_got[2].astype(F32)
    ).astype(BF16)
    collect(stage_v, got_v, vg_copies, vgrad_ref)

    wgrad_ref[...] = dwp[here]

    def last_right():
        right_copy(here).wait_recv()
        wgrad_ref[...] += sum_got[here + 1].astype(F32)

    def last_left():
        left_copy(here).wait_recv()
        wgrad_ref[...] += sum_got[here].astype(F32)

    pl.when(not_first)(last_right)
    pl.when(not_last)(last_left)

    for c in gg_copies + vg_copies:
        c.wait_send()
    for c in (cot_core, cot_side, cot_next, out_far, out_core, out_side):
        c.wait_send()
    each(later, lambda e: states(end_f, planes_f, "fwd", e, True).wait_send())
    each(earlier, lambda e: states(end_b, planes_b, "bwd", e, False).wait_send())
    for e in range(outer):
        pl.when(jnp.logical_and(not_last, here >= e))(
            lambda e=e: w_right(e, wbuf.at[e]).wait_send()
        )
        pl.when(jnp.logical_and(not_first, here <= e))(
            lambda e=e: w_left(e, wbuf.at[e]).wait_send()
        )
        pl.when(here < e)(lambda e=e: right_copy(e).wait_send())
        pl.when(here > e)(lambda e=e: left_copy(e).wait_send())
    assert sum(s for _, s in spots.values()) <= send_sems.shape[0]


def per_device(values, gating, out_weight, residue, decay_rate, skip_gain, cotangent):
    tokens, width = values.shape
    ctx = lax.axis_size("ctx")
    outer = ctx // INNER
    modes = decay_rate.shape[1]
    lanes = width // ctx
    rows = out_weight.shape[0]
    span = tokens * INNER
    quarter = (INNER, outer, tokens, lanes)
    chans = (outer, INNER, tokens, lanes)
    state = (outer, modes, lanes)
    slots = (outer, rows, width)
    scratch = [
        ((outer, 1, modes), F32), ((outer, modes, 128), F32), (state, F32),
        (quarter, BF16), (quarter, BF16), (chans, BF16), (chans, BF16),
        ((INNER, tokens, width), BF16), (slots, BF16), ((outer, B, lanes), F32),
        ((outer, span, lanes), F32), ((outer, span // B, modes, lanes), F32),
        ((outer, span, lanes), F32), ((span, outer * lanes), BF16), ((span, lanes), F32), ((B + 8, lanes), F32),
        (state, BF16), (state, BF16), ((outer,) + state, BF16), ((outer,) + state, BF16),
        (quarter, BF16), (quarter, BF16),
        ((INNER, tokens, width), F32), ((3, tokens, width), BF16), ((3, tokens, width), BF16),
        (slots, F32), ((outer + 1, rows, width), BF16), (slots, BF16),
    ]
    sems = pltpu.SemaphoreType.DMA((18 + 9 * outer,))
    args = (values, gating, out_weight, cotangent, residue, decay_rate, skip_gain.reshape(ctx, lanes))
    out = jax.ShapeDtypeStruct((tokens, width), BF16)
    macs = 3 * span * outer * lanes * width
    return pl.pallas_call(
        functools.partial(kernel, outer),
        out_shape=[out, out, out, jax.ShapeDtypeStruct((rows, width), F32)],
        in_specs=[pl.BlockSpec(memory_space=pltpu.VMEM)] * len(args),
        out_specs=[pl.BlockSpec(memory_space=pltpu.VMEM)] * 4,
        scratch_shapes=[pltpu.VMEM(s, d) for s, d in scratch] + [sems, sems],
        compiler_params=pltpu.CompilerParams(
            collective_id=0, has_side_effects=True, vmem_limit_bytes=61 * 2**20
        ),
        cost_estimate=pl.CostEstimate(
            flops=2 * macs, bytes_accessed=6 * 2**20, transcendentals=0
        ),
    )(*args)


def solution(mesh):
    rows = P(("parts", "ctx"), None)
    return jax.shard_map(
        per_device,
        mesh=mesh,
        in_specs=(rows, rows, rows, P("parts", None), P("parts", None), P("parts"), rows),
        out_specs=(rows,) * 4,
        check_vma=False,
    )
```

```python
import functools

import jax
import jax.numpy as jnp
from jax import lax
from jax.experimental import pallas as pl
from jax.experimental.pallas import tpu as pltpu
from jax.sharding import PartitionSpec as P

B = 64
F32 = jnp.float32
BF16 = jnp.bfloat16


def dot(a, b):
    return jnp.dot(a, b, preferred_element_type=F32)


def split(a):
    hi = a.astype(BF16)
    return hi, (a - hi.astype(F32)).astype(BF16)


def dot3(a, b):
    ah, al = a
    bh, bl = split(b)
    return dot(ah, bh) + dot(ah, bl) + dot(al, bh)


def iota(shape, dim):
    return lax.broadcasted_iota(jnp.int32, shape, dim).astype(F32)


def make_tables(
    res_ref, rate_ref, skip_ref, row_ref, col_ref, rest_ref, taps_ref, seq_total, outer, mine
):
    _, modes, lanes = rest_ref.shape
    for g in range(outer):
        block = g * INNER + mine
        group = block * rate_ref.shape[0] // (outer * INNER)
        row_ref[g] = rate_ref[pl.ds(group, 1), :] / seq_total
        col_ref[g] = jnp.broadcast_to(row_ref[g], (128, modes)).T
        chans = pl.ds(pl.multiple_of(block * lanes, lanes), lanes)
        if res_ref.shape[0] == modes:
            rest_ref[g] = res_ref[:, chans]
        else:
            rest_ref[g] = res_ref[chans, :].T
        lag_pow = jnp.exp(-iota((B, modes), 0) * row_ref[g])
        taps = jnp.dot(
            lag_pow, rest_ref[g], preferred_element_type=F32, precision=lax.Precision.HIGHEST
        )
        first = (lax.broadcasted_iota(jnp.int32, taps.shape, 0) == 0).astype(F32)
        taps_ref[g] = taps + first * skip_ref[pl.ds(block, 1), :]


def ends_part(get, col_ref, ends_ref, g, blocks, back):
    modes = col_ref.shape[1]
    offs = iota((modes, B), 1)
    powers = jnp.exp(-(offs if back else B - 1.0 - offs) * col_ref[g][:, :B])
    powers = split(powers)

    def body(b, carry):
        x = get(b)
        if x.dtype == BF16:
            ends_ref[g, b] = dot(powers[0], x) + dot(powers[1], x)
        else:
            ends_ref[g, b] = dot3(powers, x)
        return carry

    lax.fori_loop(0, blocks, body, 0)


def inner_part(get, taps_ref, inner_ref, pad_ref, g, blocks, back, lanes):
    zeros = jnp.zeros((8, lanes), F32)
    if back:
        pad_ref[B : B + 8, :] = zeros
    else:
        pad_ref[0:8, :] = zeros

    def body(b, carry):
        xf = get(b).astype(F32)
        if back:
            pad_ref[0:B, :] = xf
        else:
            pad_ref[8 : B + 8, :] = xf
        acc = [jnp.zeros((8, lanes), F32) for _ in range(B // 8)]
        for low in range(8):
            if low == 0:
                shifted = xf
            elif back:
                shifted = pad_ref[low : B + low, :]
            else:
                shifted = pad_ref[8 - low : B + 8 - low, :]
            for high in range(B // 8):
                k = 8 * high + low
                tap = taps_ref[g, k : k + 1, :]
                for r in range(B // 8 - high):
                    if back:
                        acc[r] = acc[r] + tap * shifted[8 * (r + high) : 8 * (r + high) + 8]
                    else:
                        acc[r + high] = acc[r + high] + tap * shifted[8 * r : 8 * r + 8]
        inner_ref[g, pl.ds(pl.multiple_of(b * B, B), B), :] = jnp.concatenate(acc, axis=0)
        return carry

    lax.fori_loop(0, blocks, body, 0)


def plane_end(ends_ref, col_ref, g, blocks, back):
    total = ends_ref[g, blocks - 1 if back else 0]
    step = jnp.exp(-float(B) * col_ref[g][:, : total.shape[1]])
    for i in range(1, blocks):
        total = step * total + ends_ref[g, blocks - 1 - i if back else i]
    return total


def finish(state, put, rest_ref, row_ref, col_ref, inner_ref, ends_ref, g, blocks, back):
    modes = col_ref.shape[1]
    offs = iota((B, modes), 0)
    lead = split(jnp.exp(-(B - offs if back else offs + 1.0) * row_ref[g]))
    step = jnp.exp(-float(B) * col_ref[g][:, : state.shape[1]])
    for i in range(blocks):
        b = blocks - 1 - i if back else i
        cross = dot3(lead, state * rest_ref[g])
        put(b, inner_ref[g, b * B : (b + 1) * B, :] + cross)
        state = step * state + ends_ref[g, b]


def incoming(planes_ref, col_ref, g, outer, here, span, back):
    state = jnp.zeros(planes_ref.shape[2:], F32)
    step = jnp.exp(-float(span) * col_ref[g][:, : state.shape[1]])
    for i in range(outer - 1):
        e = outer - 1 - i if back else i
        use = e > here if back else e < here
        state = jnp.where(use, step * state + planes_ref[e, g].astype(F32), state)
    return state


INNER = 4


def kernel(
    outer, val_ref, gat_ref, w_ref, cot_ref, res_ref, rate_ref, skip_ref,
    out_ref, vgrad_ref, ggrad_ref, wgrad_ref,
    row_ref, col_ref, rest_ref, stage_v, stage_g, x, gate, cots, wbuf, taps, inner, ends, conv, mixed, grad, pad,
    end_f, end_b, planes_f, planes_b, got_g, got_v, outp, out_send, out_got,
    dwp, sum_got, sum_send, send_sems, recv_sems,
):
    tokens, width = val_ref.shape
    groups, modes, lanes = rest_ref.shape
    span = tokens * INNER
    blocks = span // B
    per = tokens // B
    me = lax.axis_index("ctx")
    here, mine = me // INNER, lax.rem(me, INNER)
    hi, lo = mine // 2, lax.rem(mine, 2)
    peers = (hi * 2 + 1 - lo, (1 - hi) * 2 + lo, (1 - hi) * 2 + 1 - lo)
    core, side, far = peers
    not_first, not_last = here > 0, here < outer - 1

    spots = {}

    def sem(name, index=0, size=1):
        if name not in spots:
            spots[name] = sum(s for _, s in spots.values()), size
        return spots[name][0] + index

    def rdma(src, dst, name, index, size, plane, q, recv=None):
        spot = sem(name, index, size)
        got = spot if recv is None else sem(recv[0], recv[1], recv[2])
        return pltpu.make_async_remote_copy(
            src_ref=src, dst_ref=dst, send_sem=send_sems.at[spot], recv_sem=recv_sems.at[got],
            device_id={"ctx": plane * INNER + q}, device_id_type=pl.DeviceIdType.MESH,
        )

    barrier = pltpu.get_barrier_semaphore()
    for q in peers:
        pl.semaphore_signal(
            barrier, inc=1, device_id={"ctx": here * INNER + q},
            device_id_type=pl.DeviceIdType.MESH,
        )
    for d in range(1, outer):
        plane = lax.rem(here + d, outer)
        pl.semaphore_signal(
            barrier, inc=1, device_id={"ctx": plane * INNER + mine},
            device_id_type=pl.DeviceIdType.MESH,
        )
    pl.semaphore_wait(barrier, INNER - 1 + outer - 1)

    def w_right(slot, src):
        return rdma(src, wbuf.at[slot], "w_right", slot, outer, here + 1, mine,
                    ("w", slot, outer))

    def w_left(slot, src):
        return rdma(src, wbuf.at[slot], "w_left", slot, outer, here - 1, mine,
                    ("w", slot, outer))

    sem("w", 0, outer)
    pl.when(not_last)(lambda: w_right(here, w_ref).start())
    pl.when(not_first)(lambda: w_left(here, w_ref).start())

    def w_step(k):
        def from_left():
            slot = here - k
            w_right(slot, wbuf.at[slot]).wait_recv()
            pl.when(not_last)(lambda: w_right(slot, wbuf.at[slot]).start())

        def from_right():
            slot = here + k
            w_left(slot, wbuf.at[slot]).wait_recv()
            pl.when(not_first)(lambda: w_left(slot, wbuf.at[slot]).start())

        pl.when(here - k >= 0)(from_left)
        pl.when(here + k < outer)(from_right)

    def to_channels(stage, dst, name, src):
        if src is not None:
            for q in range(INNER):
                for z in range(outer):
                    at = (z * INNER + q) * lanes
                    stage[q, z] = src[:, at : at + lanes]
        copies = [
            rdma(stage.at[q], dst.at[:, mine], name, i, 3, here, q) for i, q in enumerate(peers)
        ]
        if src is not None:
            for c in copies:
                c.start()
            dst[:, pl.ds(mine, 1)] = stage[pl.ds(mine, 1)].reshape(outer, 1, tokens, lanes)
        return copies

    val_copies = to_channels(stage_v, x, "values", val_ref)
    cot_core = rdma(cot_ref, cots.at[mine], "cot", 0, 3, here, core)
    cot_side = rdma(cot_ref, cots.at[mine], "cot", 1, 3, here, side)
    cot_next = rdma(cots.at[side], cots.at[side], "cot", 2, 3, here, core)
    cot_core.start()
    make_tables(
        res_ref, rate_ref, skip_ref, row_ref, col_ref, rest_ref, taps,
        float(tokens * outer * INNER), outer, mine,
    )
    gat_copies = to_channels(stage_g, gate, "gating", gat_ref)
    wbuf[pl.ds(here, 1)] = w_ref[...].reshape(1, w_ref.shape[0], width)
    cots[pl.ds(mine, 1)] = cot_ref[...].reshape(1, tokens, width)

    for c in val_copies:
        c.wait_recv()
    cot_side.start()

    def forward_group(inside, g, carry):
        def get(b):
            return x[g, b // per, pl.ds(pl.multiple_of(lax.rem(b, per) * B, B), B), :]

        if inside:
            inner_part(get, taps, inner, pad, g, blocks, False, lanes)
        else:
            ends_part(get, col_ref, ends, g, blocks, False)
            end_f[g] = plane_end(ends, col_ref, g, blocks, False).astype(BF16)
        return carry

    lax.fori_loop(0, groups, functools.partial(forward_group, False), 0)

    def states(end, planes, name, e, upward):
        return rdma(end, planes.at[here], name, e, outer, e, mine, (name + "_got", here, outer))

    def states_got(end, planes, name, e):
        return rdma(end, planes.at[e], name, e, outer, e, mine, (name + "_got", e, outer))

    def each(planes_of, act):
        for e in range(outer):
            pl.when(planes_of(e))(functools.partial(act, e))

    sem("fwd", 0, outer)
    sem("fwd_got", 0, outer)
    sem("bwd", 0, outer)
    sem("bwd_got", 0, outer)
    later = lambda e: here < e
    earlier = lambda e: here > e
    each(later, lambda e: states(end_f, planes_f, "fwd", e, True).start())
    lax.fori_loop(0, groups, functools.partial(forward_group, True), 0)
    w_step(1)
    for c in gat_copies:
        c.wait_recv()
    each(earlier, lambda e: states_got(end_f, planes_f, "fwd", e).wait_recv())
    for g in range(groups):
        def put(b, value):
            rows = slice((b % per) * B, (b % per + 1) * B)
            conv[g, b * B : (b + 1) * B, :] = value
            m = (gate[g, b // per, rows, :].astype(F32) * value).astype(BF16)
            mixed[b * B : (b + 1) * B, g * lanes : (g + 1) * lanes] = m

        state = incoming(planes_f, col_ref, g, outer, here, span, False)
        finish(state, put, rest_ref, row_ref, col_ref, inner, ends, g, blocks, False)

    cot_side.wait_recv()
    cot_next.start()
    for k in range(2, outer - 1):
        w_step(k)
    cot_core.wait_recv()
    cot_next.wait_recv()


    def right_copy(e):
        return rdma(sum_send.at[e], sum_got.at[e + 1], "sum_right", e, outer, here + 1, mine)

    def left_copy(e):
        return rdma(sum_send.at[e], sum_got.at[e], "sum_left", e, outer, here - 1, mine)

    def start_right(e):
        sum_send[e] = dwp[e].astype(BF16)
        right_copy(e).start()

    def start_left(e):
        sum_send[e] = dwp[e].astype(BF16)
        left_copy(e).start()

    def pass_right(e):
        right_copy(e).wait_recv()
        sum_send[e] = (dwp[e] + sum_got[e + 1].astype(F32)).astype(BF16)
        right_copy(e).start()

    def pass_left(e):
        left_copy(e).wait_recv()
        sum_send[e] = (dwp[e] + sum_got[e].astype(F32)).astype(BF16)
        left_copy(e).start()

    def weight_terms(order, end, start):
        for g in order:
            dwp[g] = lax.dot_general(
                mixed[:, g * lanes : (g + 1) * lanes], cots[...].reshape(span, width),
                (((0,), (0,)), ((), ())), preferred_element_type=F32,
            )
            if g != end:
                pl.when(here == end)(functools.partial(start, g))

    lower = here < outer // 2
    upper = here >= outer // 2
    pl.when(lower)(lambda: weight_terms(range(outer)[::-1], 0, start_right))
    pl.when(upper)(lambda: weight_terms(range(outer), outer - 1, start_left))

    def sum_step(k, near):
        e, f = outer - k, k - 1
        right = jnp.logical_and(not_first, here < e)
        left = jnp.logical_and(not_last, here > f)
        pl.when(jnp.logical_and(lower if near else upper, right))(functools.partial(pass_right, e))
        pl.when(jnp.logical_and(upper if near else lower, left))(functools.partial(pass_left, f))

    for c in val_copies + gat_copies:
        c.wait_send()

    def backward_group(g):
        grad[...] = lax.dot_general(
            cots[...].reshape(span, width), wbuf[g], (((1,), (1,)), ((), ())),
            preferred_element_type=F32,
        )

        def get(b):
            rows = pl.ds(pl.multiple_of(b * B, B), B)
            sub = pl.ds(pl.multiple_of(lax.rem(b, per) * B, B), B)
            part = grad[rows, :]
            stage_g[b // per, g, sub, :] = (part * conv[g, rows, :]).astype(BF16)
            signal_back = part * gate[g, b // per, sub, :].astype(F32)
            inner[g, rows, :] = signal_back
            return signal_back

        ends_part(get, col_ref, ends, g, blocks, True)
        end_b[g] = plane_end(ends, col_ref, g, blocks, True).astype(BF16)
        each(earlier, lambda e: rdma(
            end_b.at[g], planes_b.at[here, g], "bwd", e, outer, e, mine, ("bwd_got", here, outer)
        ).start())

        def again(b):
            return inner[g, pl.ds(pl.multiple_of(b * B, B), B), :]

        inner_part(again, taps, inner, pad, g, blocks, True, lanes)

    backward_group(here)

    def around(k, carry):
        pl.when(k == outer - 1)(lambda: w_step(outer - 1))
        pl.when(here - k >= 0)(lambda: backward_group(here - k))
        pl.when(here + k < outer)(lambda: backward_group(here + k))
        pl.when(k == 1)(lambda: sum_step(1, True))
        return carry

    lax.fori_loop(1, outer, around, 0)
    def to_tokens(buf, got, name):
        return [
            rdma(buf.at[q], got.at[mine], name, i, 3, here, q) for i, q in enumerate(peers)
        ]

    gg_copies = to_tokens(stage_g, got_g, "gate_grad")
    vg_copies = to_tokens(stage_v, got_v, "value_grad")
    for c in gg_copies:
        c.start()

    weight_rows = groups * w_ref.shape[0]
    chunk = min(512, width)

    def out_term(j, carry):
        cols = pl.ds(pl.multiple_of(j * chunk, chunk), chunk)
        part = dot(mixed[...], wbuf[:, :, cols].reshape(weight_rows, chunk))
        outp[:, :, cols] = part.reshape(INNER, tokens, chunk)
        return carry

    lax.fori_loop(0, width // chunk, out_term, 0)
    out_far = rdma(out_send.at[0], out_got.at[0], "out", 0, 3, here, core)
    out_core = rdma(out_send.at[1], out_got.at[1], "out", 1, 3, here, core)
    out_side = rdma(out_send.at[2], out_got.at[2], "out", 2, 3, here, side)
    out_send[0] = outp[far].astype(BF16)
    out_far.start()
    out_send[1] = outp[core].astype(BF16)
    out_core.start()
    for k in range(2, outer):
        sum_step(k, True)
    out_far.wait_recv()
    out_send[2] = (outp[side] + out_got[0].astype(F32)).astype(BF16)
    out_side.start()

    each(later, lambda e: states_got(end_b, planes_b, "bwd", e).wait_recv())
    for g in range(groups):
        def put(b, value):
            rows = slice((b % per) * B, (b % per + 1) * B)
            stage_v[b // per, g, rows, :] = value.astype(BF16)

        state = incoming(planes_b, col_ref, g, outer, here, span, True)
        finish(state, put, rest_ref, row_ref, col_ref, inner, ends, g, blocks, True)
    for c in vg_copies:
        c.start()
    for k in range(1, outer):
        sum_step(k, False)

    def collect(buf, got, copies, dst):
        got[pl.ds(mine, 1)] = buf[pl.ds(mine, 1)]
        for c in copies:
            c.wait_recv()
        for q in range(INNER):
            for z in range(outer):
                at = (z * INNER + q) * lanes
                dst[:, at : at + lanes] = got[q, z]

    collect(stage_g, got_g, gg_copies, ggrad_ref)
    out_core.wait_recv()
    out_side.wait_recv()
    out_ref[...] = (
        outp[mine] + out_got[1].astype(F32) + out_got[2].astype(F32)
    ).astype(BF16)
    collect(stage_v, got_v, vg_copies, vgrad_ref)

    wgrad_ref[...] = dwp[here]

    def last_right():
        right_copy(here).wait_recv()
        wgrad_ref[...] += sum_got[here + 1].astype(F32)

    def last_left():
        left_copy(here).wait_recv()
        wgrad_ref[...] += sum_got[here].astype(F32)

    pl.when(not_first)(last_right)
    pl.when(not_last)(last_left)

    for c in gg_copies + vg_copies:
        c.wait_send()
    for c in (cot_core, cot_side, cot_next, out_far, out_core, out_side):
        c.wait_send()
    each(later, lambda e: states(end_f, planes_f, "fwd", e, True).wait_send())
    each(earlier, lambda e: states(end_b, planes_b, "bwd", e, False).wait_send())
    for e in range(outer):
        pl.when(jnp.logical_and(not_last, here >= e))(
            lambda e=e: w_right(e, wbuf.at[e]).wait_send()
        )
        pl.when(jnp.logical_and(not_first, here <= e))(
            lambda e=e: w_left(e, wbuf.at[e]).wait_send()
        )
        pl.when(here < e)(lambda e=e: right_copy(e).wait_send())
        pl.when(here > e)(lambda e=e: left_copy(e).wait_send())
    assert sum(s for _, s in spots.values()) <= send_sems.shape[0]


def per_device(values, gating, out_weight, residue, decay_rate, skip_gain, cotangent):
    tokens, width = values.shape
    ctx = lax.axis_size("ctx")
    outer = ctx // INNER
    modes = decay_rate.shape[1]
    lanes = width // ctx
    rows = out_weight.shape[0]
    span = tokens * INNER
    quarter = (INNER, outer, tokens, lanes)
    chans = (outer, INNER, tokens, lanes)
    state = (outer, modes, lanes)
    slots = (outer, rows, width)
    scratch = [
        ((outer, 1, modes), F32), ((outer, modes, 128), F32), (state, F32),
        (quarter, BF16), (quarter, BF16), (chans, BF16), (chans, BF16),
        ((INNER, tokens, width), BF16), (slots, BF16), ((outer, B, lanes), F32),
        ((outer, span, lanes), F32), ((outer, span // B, modes, lanes), F32),
        ((outer, span, lanes), F32), ((span, outer * lanes), BF16), ((span, lanes), F32), ((B + 8, lanes), F32),
        (state, BF16), (state, BF16), ((outer,) + state, BF16), ((outer,) + state, BF16),
        (quarter, BF16), (quarter, BF16),
        ((INNER, tokens, width), F32), ((3, tokens, width), BF16), ((3, tokens, width), BF16),
        (slots, F32), ((outer + 1, rows, width), BF16), (slots, BF16),
    ]
    sems = pltpu.SemaphoreType.DMA((18 + 9 * outer,))
    table = residue.T if lanes % 128 == 0 else residue
    args = (values, gating, out_weight, cotangent, table, decay_rate, skip_gain.reshape(ctx, lanes))
    out = jax.ShapeDtypeStruct((tokens, width), BF16)
    macs = 3 * span * outer * lanes * width
    results = pl.pallas_call(
        functools.partial(kernel, outer),
        out_shape=[out, out, out, jax.ShapeDtypeStruct((rows, width), F32)],
        in_specs=[pl.BlockSpec(memory_space=pltpu.VMEM)] * len(args),
        out_specs=[pl.BlockSpec(memory_space=pltpu.VMEM)] * 4,
        scratch_shapes=[pltpu.VMEM(s, d) for s, d in scratch] + [sems, sems],
        compiler_params=pltpu.CompilerParams(
            collective_id=0, has_side_effects=True, vmem_limit_bytes=61 * 2**20
        ),
        cost_estimate=pl.CostEstimate(
            flops=2 * macs, bytes_accessed=6 * 2**20, transcendentals=0
        ),
    )(*args)
    whole = [pl.BlockSpec(memory_space=pltpu.HBM)] * 4
    return pl.pallas_call(
        hand_over,
        out_shape=[jax.ShapeDtypeStruct(r.shape, r.dtype) for r in results],
        in_specs=whole,
        out_specs=whole,
        scratch_shapes=[pltpu.SemaphoreType.DMA((4,))],
    )(*results)


def hand_over(*refs):
    copies = [
        pltpu.make_async_copy(refs[i], refs[4 + i], refs[8].at[i]) for i in range(4)
    ]
    for c in copies:
        c.start()
    for c in copies:
        c.wait()


def solution(mesh):
    rows = P(("parts", "ctx"), None)
    return jax.shard_map(
        per_device,
        mesh=mesh,
        in_specs=(rows, rows, rows, P("parts", None), P("parts", None), P("parts"), rows),
        out_specs=(rows,) * 4,
        check_vma=False,
    )
```

```python
import functools

import jax
import jax.numpy as jnp
from jax import lax
from jax.experimental import pallas as pl
from jax.experimental.pallas import tpu as pltpu
from jax.sharding import PartitionSpec as P

B = 64
F32 = jnp.float32
BF16 = jnp.bfloat16


def dot(a, b):
    return jnp.dot(a, b, preferred_element_type=F32)


def split(a):
    hi = a.astype(BF16)
    return hi, (a - hi.astype(F32)).astype(BF16)


def dot3(a, b):
    ah, al = a
    bh, bl = split(b)
    return dot(ah, bh) + dot(ah, bl) + dot(al, bh)


def iota(shape, dim):
    return lax.broadcasted_iota(jnp.int32, shape, dim).astype(F32)


def make_tables(
    res_ref, rate_ref, skip_ref, row_ref, col_ref, rest_ref, taps_ref, seq_total, outer, mine
):
    _, modes, lanes = rest_ref.shape
    for g in range(outer):
        block = g * INNER + mine
        group = block * rate_ref.shape[0] // (outer * INNER)
        row_ref[g] = rate_ref[pl.ds(group, 1), :] / seq_total
        col_ref[g] = jnp.broadcast_to(row_ref[g], (128, modes)).T
        chans = pl.ds(pl.multiple_of(block * lanes, lanes), lanes)
        if res_ref.shape[0] == modes:
            rest_ref[g] = res_ref[:, chans]
        else:
            rest_ref[g] = res_ref[chans, :].T
        lag_pow = jnp.exp(-iota((B, modes), 0) * row_ref[g])
        taps = jnp.dot(
            lag_pow, rest_ref[g], preferred_element_type=F32, precision=lax.Precision.HIGHEST
        )
        first = (lax.broadcasted_iota(jnp.int32, taps.shape, 0) == 0).astype(F32)
        taps_ref[g] = taps + first * skip_ref[pl.ds(block, 1), :]


def ends_part(get, col_ref, ends_ref, g, blocks, back):
    modes = col_ref.shape[1]
    offs = iota((modes, B), 1)
    powers = jnp.exp(-(offs if back else B - 1.0 - offs) * col_ref[g][:, :B])
    powers = split(powers)

    def body(b, carry):
        x = get(b)
        if x.dtype == BF16:
            ends_ref[g, b] = dot(powers[0], x) + dot(powers[1], x)
        else:
            ends_ref[g, b] = dot3(powers, x)
        return carry

    lax.fori_loop(0, blocks, body, 0)


def inner_part(get, taps_ref, inner_ref, pad_ref, g, blocks, back, lanes):
    zeros = jnp.zeros((8, lanes), F32)
    if back:
        pad_ref[B : B + 8, :] = zeros
    else:
        pad_ref[0:8, :] = zeros

    def body(b, carry):
        xf = get(b).astype(F32)
        if back:
            pad_ref[0:B, :] = xf
        else:
            pad_ref[8 : B + 8, :] = xf
        acc = [jnp.zeros((8, lanes), F32) for _ in range(B // 8)]
        for low in range(8):
            if low == 0:
                shifted = xf
            elif back:
                shifted = pad_ref[low : B + low, :]
            else:
                shifted = pad_ref[8 - low : B + 8 - low, :]
            for high in range(B // 8):
                k = 8 * high + low
                tap = taps_ref[g, k : k + 1, :]
                for r in range(B // 8 - high):
                    if back:
                        acc[r] = acc[r] + tap * shifted[8 * (r + high) : 8 * (r + high) + 8]
                    else:
                        acc[r + high] = acc[r + high] + tap * shifted[8 * r : 8 * r + 8]
        inner_ref[g, pl.ds(pl.multiple_of(b * B, B), B), :] = jnp.concatenate(acc, axis=0)
        return carry

    lax.fori_loop(0, blocks, body, 0)


def plane_end(ends_ref, col_ref, g, blocks, back):
    total = ends_ref[g, blocks - 1 if back else 0]
    step = jnp.exp(-float(B) * col_ref[g][:, : total.shape[1]])
    for i in range(1, blocks):
        total = step * total + ends_ref[g, blocks - 1 - i if back else i]
    return total


def finish(state, put, rest_ref, row_ref, col_ref, inner_ref, ends_ref, g, blocks, back):
    modes = col_ref.shape[1]
    offs = iota((B, modes), 0)
    lead = split(jnp.exp(-(B - offs if back else offs + 1.0) * row_ref[g]))
    step = jnp.exp(-float(B) * col_ref[g][:, : state.shape[1]])
    for i in range(blocks):
        b = blocks - 1 - i if back else i
        cross = dot3(lead, state * rest_ref[g])
        put(b, inner_ref[g, b * B : (b + 1) * B, :] + cross)
        state = step * state + ends_ref[g, b]


def incoming(planes_ref, col_ref, g, outer, here, span, back):
    state = jnp.zeros(planes_ref.shape[2:], F32)
    step = jnp.exp(-float(span) * col_ref[g][:, : state.shape[1]])
    for i in range(outer - 1):
        e = outer - 1 - i if back else i
        use = e > here if back else e < here
        state = jnp.where(use, step * state + planes_ref[e, g].astype(F32), state)
    return state


INNER = 4


def kernel(
    outer, val_ref, gat_ref, w_ref, cot_ref, res_ref, rate_ref, skip_ref,
    out_ref, vgrad_ref, ggrad_ref, wgrad_ref,
    row_ref, col_ref, rest_ref, stage_v, stage_g, x, gate, cots, wbuf, taps, inner, ends, conv, mixed, grad, pad,
    end_f, end_b, planes_f, planes_b, got_g, got_v, outp, out_send, out_got,
    dwp, sum_got, sum_send, send_sems, recv_sems,
):
    tokens, width = val_ref.shape
    groups, modes, lanes = rest_ref.shape
    span = tokens * INNER
    blocks = span // B
    per = tokens // B
    me = lax.axis_index("ctx")
    here, mine = me // INNER, lax.rem(me, INNER)
    hi, lo = mine // 2, lax.rem(mine, 2)
    peers = (hi * 2 + 1 - lo, (1 - hi) * 2 + lo, (1 - hi) * 2 + 1 - lo)
    core, side, far = peers
    not_first, not_last = here > 0, here < outer - 1

    spots = {}

    def sem(name, index=0, size=1):
        if name not in spots:
            spots[name] = sum(s for _, s in spots.values()), size
        return spots[name][0] + index

    def rdma(src, dst, name, index, size, plane, q, recv=None):
        spot = sem(name, index, size)
        got = spot if recv is None else sem(recv[0], recv[1], recv[2])
        return pltpu.make_async_remote_copy(
            src_ref=src, dst_ref=dst, send_sem=send_sems.at[spot], recv_sem=recv_sems.at[got],
            device_id={"ctx": plane * INNER + q}, device_id_type=pl.DeviceIdType.MESH,
        )

    barrier = pltpu.get_barrier_semaphore()
    for q in peers:
        pl.semaphore_signal(
            barrier, inc=1, device_id={"ctx": here * INNER + q},
            device_id_type=pl.DeviceIdType.MESH,
        )
    for d in range(1, outer):
        plane = lax.rem(here + d, outer)
        pl.semaphore_signal(
            barrier, inc=1, device_id={"ctx": plane * INNER + mine},
            device_id_type=pl.DeviceIdType.MESH,
        )
    pl.semaphore_wait(barrier, INNER - 1 + outer - 1)

    def w_right(slot, src):
        return rdma(src, wbuf.at[slot], "w_right", slot, outer, here + 1, mine,
                    ("w", slot, outer))

    def w_left(slot, src):
        return rdma(src, wbuf.at[slot], "w_left", slot, outer, here - 1, mine,
                    ("w", slot, outer))

    sem("w", 0, outer)
    pl.when(not_last)(lambda: w_right(here, w_ref).start())
    pl.when(not_first)(lambda: w_left(here, w_ref).start())

    def w_step(k):
        def from_left():
            slot = here - k
            w_right(slot, wbuf.at[slot]).wait_recv()
            pl.when(not_last)(lambda: w_right(slot, wbuf.at[slot]).start())

        def from_right():
            slot = here + k
            w_left(slot, wbuf.at[slot]).wait_recv()
            pl.when(not_first)(lambda: w_left(slot, wbuf.at[slot]).start())

        pl.when(here - k >= 0)(from_left)
        pl.when(here + k < outer)(from_right)

    def to_channels(stage, dst, name, src):
        if src is not None:
            for q in range(INNER):
                for z in range(outer):
                    at = (z * INNER + q) * lanes
                    stage[q, z] = src[:, at : at + lanes]
        copies = [
            rdma(stage.at[q], dst.at[:, mine], name, i, 3, here, q) for i, q in enumerate(peers)
        ]
        if src is not None:
            for c in copies:
                c.start()
            dst[:, pl.ds(mine, 1)] = stage[pl.ds(mine, 1)].reshape(outer, 1, tokens, lanes)
        return copies

    val_copies = to_channels(stage_v, x, "values", val_ref)
    cot_core = rdma(cot_ref, cots.at[mine], "cot", 0, 1, here, core)
    half = width // 2
    halves = [slice(h * half, (h + 1) * half) for h in range(2)]
    cot_side = [
        rdma(cot_ref.at[:, c], cots.at[mine, :, c], "cot_side", h, 2, here, side)
        for h, c in enumerate(halves)
    ]
    cot_next = [
        rdma(cots.at[side, :, c], cots.at[side, :, c], "cot_next", h, 2, here, core)
        for h, c in enumerate(halves)
    ]
    cot_core.start()
    make_tables(
        res_ref, rate_ref, skip_ref, row_ref, col_ref, rest_ref, taps,
        float(tokens * outer * INNER), outer, mine,
    )
    gat_copies = to_channels(stage_g, gate, "gating", gat_ref)
    wbuf[pl.ds(here, 1)] = w_ref[...].reshape(1, w_ref.shape[0], width)
    cots[pl.ds(mine, 1)] = cot_ref[...].reshape(1, tokens, width)

    for c in val_copies:
        c.wait_recv()
    cot_side[0].start()

    def forward_group(inside, g, carry):
        def get(b):
            return x[g, b // per, pl.ds(pl.multiple_of(lax.rem(b, per) * B, B), B), :]

        if inside:
            inner_part(get, taps, inner, pad, g, blocks, False, lanes)
        else:
            ends_part(get, col_ref, ends, g, blocks, False)
            end_f[g] = plane_end(ends, col_ref, g, blocks, False).astype(BF16)
        return carry

    lax.fori_loop(0, groups, functools.partial(forward_group, False), 0)

    def states(end, planes, name, e, upward):
        return rdma(end, planes.at[here], name, e, outer, e, mine, (name + "_got", here, outer))

    def states_got(end, planes, name, e):
        return rdma(end, planes.at[e], name, e, outer, e, mine, (name + "_got", e, outer))

    def each(planes_of, act):
        for e in range(outer):
            pl.when(planes_of(e))(functools.partial(act, e))

    sem("fwd", 0, outer)
    sem("fwd_got", 0, outer)
    sem("bwd", 0, outer)
    sem("bwd_got", 0, outer)
    later = lambda e: here < e
    earlier = lambda e: here > e
    each(later, lambda e: states(end_f, planes_f, "fwd", e, True).start())
    lax.fori_loop(0, groups, functools.partial(forward_group, True), 0)
    w_step(1)
    cot_side[1].start()
    for c in gat_copies:
        c.wait_recv()
    each(earlier, lambda e: states_got(end_f, planes_f, "fwd", e).wait_recv())
    for g in range(groups):
        def put(b, value):
            rows = slice((b % per) * B, (b % per + 1) * B)
            conv[g, b * B : (b + 1) * B, :] = value
            m = (gate[g, b // per, rows, :].astype(F32) * value).astype(BF16)
            mixed[b * B : (b + 1) * B, g * lanes : (g + 1) * lanes] = m

        state = incoming(planes_f, col_ref, g, outer, here, span, False)
        finish(state, put, rest_ref, row_ref, col_ref, inner, ends, g, blocks, False)

    cot_side[0].wait_recv()
    cot_next[0].start()
    for k in range(2, outer - 1):
        w_step(k)
    cot_core.wait_recv()
    cot_next[0].wait_recv()


    def right_copy(e, h):
        return rdma(sum_send.at[e, :, halves[h]], sum_got.at[e + 1, :, halves[h]],
                    "sum_right", e * 2 + h, 2 * outer, here + 1, mine)

    def left_copy(e, h):
        return rdma(sum_send.at[e, :, halves[h]], sum_got.at[e, :, halves[h]],
                    "sum_left", e * 2 + h, 2 * outer, here - 1, mine)

    def start_right(e, h):
        c = halves[h]
        sum_send[e, :, c] = dwp[e, :, c].astype(BF16)
        right_copy(e, h).start()

    def start_left(e, h):
        c = halves[h]
        sum_send[e, :, c] = dwp[e, :, c].astype(BF16)
        left_copy(e, h).start()

    def pass_right(e, h):
        c = halves[h]
        right_copy(e, h).wait_recv()
        sum_send[e, :, c] = (dwp[e, :, c] + sum_got[e + 1, :, c].astype(F32)).astype(BF16)
        right_copy(e, h).start()

    def pass_left(e, h):
        c = halves[h]
        left_copy(e, h).wait_recv()
        sum_send[e, :, c] = (dwp[e, :, c] + sum_got[e, :, c].astype(F32)).astype(BF16)
        left_copy(e, h).start()

    def weight_terms(order, end, start, h):
        for g in order:
            dwp[g, :, halves[h]] = lax.dot_general(
                mixed[:, g * lanes : (g + 1) * lanes],
                cots[:, :, halves[h]].reshape(span, half),
                (((0,), (0,)), ((), ())), preferred_element_type=F32,
            )
            if g != end:
                pl.when(here == end)(functools.partial(start, g, h))

    lower = here < outer // 2
    upper = here >= outer // 2
    for h in range(2):
        if h:
            cot_side[h].wait_recv()
            cot_next[h].start()
            cot_next[h].wait_recv()
        pl.when(lower)(lambda: weight_terms(range(outer)[::-1], 0, start_right, h))
        pl.when(upper)(lambda: weight_terms(range(outer), outer - 1, start_left, h))

    def sum_step(k, near, h):
        e, f = outer - k, k - 1
        right = jnp.logical_and(not_first, here < e)
        left = jnp.logical_and(not_last, here > f)
        pl.when(jnp.logical_and(lower if near else upper, right))(functools.partial(pass_right, e, h))
        pl.when(jnp.logical_and(upper if near else lower, left))(functools.partial(pass_left, f, h))

    for c in val_copies + gat_copies:
        c.wait_send()

    def backward_group(g):
        grad[...] = lax.dot_general(
            cots[...].reshape(span, width), wbuf[g], (((1,), (1,)), ((), ())),
            preferred_element_type=F32,
        )

        def get(b):
            rows = pl.ds(pl.multiple_of(b * B, B), B)
            sub = pl.ds(pl.multiple_of(lax.rem(b, per) * B, B), B)
            part = grad[rows, :]
            stage_g[b // per, g, sub, :] = (part * conv[g, rows, :]).astype(BF16)
            signal_back = part * gate[g, b // per, sub, :].astype(F32)
            inner[g, rows, :] = signal_back
            return signal_back

        ends_part(get, col_ref, ends, g, blocks, True)
        end_b[g] = plane_end(ends, col_ref, g, blocks, True).astype(BF16)
        each(earlier, lambda e: rdma(
            end_b.at[g], planes_b.at[here, g], "bwd", e, outer, e, mine, ("bwd_got", here, outer)
        ).start())

        def again(b):
            return inner[g, pl.ds(pl.multiple_of(b * B, B), B), :]

        inner_part(again, taps, inner, pad, g, blocks, True, lanes)

    backward_group(here)

    def around(k, carry):
        pl.when(k == outer - 1)(lambda: w_step(outer - 1))
        pl.when(here - k >= 0)(lambda: backward_group(here - k))
        pl.when(here + k < outer)(lambda: backward_group(here + k))
        pl.when(k == 1)(lambda: [sum_step(i, True, 0) for i in range(1, outer)] and None)
        return carry

    lax.fori_loop(1, outer, around, 0)
    def to_tokens(buf, got, name):
        return [
            rdma(buf.at[q], got.at[mine], name, i, 3, here, q) for i, q in enumerate(peers)
        ]

    gg_copies = to_tokens(stage_g, got_g, "gate_grad")
    vg_copies = to_tokens(stage_v, got_v, "value_grad")
    for c in gg_copies:
        c.start()

    weight_rows = groups * w_ref.shape[0]
    chunk = min(512, width)

    def out_term(j, carry):
        cols = pl.ds(pl.multiple_of(j * chunk, chunk), chunk)
        part = dot(mixed[...], wbuf[:, :, cols].reshape(weight_rows, chunk))
        outp[:, :, cols] = part.reshape(INNER, tokens, chunk)
        return carry

    lax.fori_loop(0, width // chunk, out_term, 0)
    out_far = rdma(out_send.at[0], out_got.at[0], "out", 0, 3, here, core)
    out_core = rdma(out_send.at[1], out_got.at[1], "out", 1, 3, here, core)
    out_side = rdma(out_send.at[2], out_got.at[2], "out", 2, 3, here, side)
    out_send[0] = outp[far].astype(BF16)
    out_far.start()
    out_send[1] = outp[core].astype(BF16)
    out_core.start()
    for k in range(1, outer):
        sum_step(k, True, 1)
    out_far.wait_recv()
    out_send[2] = (outp[side] + out_got[0].astype(F32)).astype(BF16)
    out_side.start()

    each(later, lambda e: states_got(end_b, planes_b, "bwd", e).wait_recv())
    for g in range(groups):
        def put(b, value):
            rows = slice((b % per) * B, (b % per + 1) * B)
            stage_v[b // per, g, rows, :] = value.astype(BF16)

        state = incoming(planes_b, col_ref, g, outer, here, span, True)
        finish(state, put, rest_ref, row_ref, col_ref, inner, ends, g, blocks, True)
    for c in vg_copies:
        c.start()
    for h in range(2):
        for k in range(1, outer):
            sum_step(k, False, h)

    def collect(buf, got, copies, dst):
        got[pl.ds(mine, 1)] = buf[pl.ds(mine, 1)]
        for c in copies:
            c.wait_recv()
        for q in range(INNER):
            for z in range(outer):
                at = (z * INNER + q) * lanes
                dst[:, at : at + lanes] = got[q, z]

    collect(stage_g, got_g, gg_copies, ggrad_ref)
    out_core.wait_recv()
    out_side.wait_recv()
    out_ref[...] = (
        outp[mine] + out_got[1].astype(F32) + out_got[2].astype(F32)
    ).astype(BF16)
    collect(stage_v, got_v, vg_copies, vgrad_ref)

    wgrad_ref[...] = dwp[here]

    def last_right():
        for h in range(2):
            right_copy(here, h).wait_recv()
        wgrad_ref[...] += sum_got[here + 1].astype(F32)

    def last_left():
        for h in range(2):
            left_copy(here, h).wait_recv()
        wgrad_ref[...] += sum_got[here].astype(F32)

    pl.when(not_first)(last_right)
    pl.when(not_last)(last_left)

    for c in gg_copies + vg_copies:
        c.wait_send()
    for c in (cot_core, *cot_side, *cot_next, out_far, out_core, out_side):
        c.wait_send()
    each(later, lambda e: states(end_f, planes_f, "fwd", e, True).wait_send())
    each(earlier, lambda e: states(end_b, planes_b, "bwd", e, False).wait_send())
    for e in range(outer):
        pl.when(jnp.logical_and(not_last, here >= e))(
            lambda e=e: w_right(e, wbuf.at[e]).wait_send()
        )
        pl.when(jnp.logical_and(not_first, here <= e))(
            lambda e=e: w_left(e, wbuf.at[e]).wait_send()
        )
        pl.when(here < e)(lambda e=e: [right_copy(e, h).wait_send() for h in range(2)] and None)
        pl.when(here > e)(lambda e=e: [left_copy(e, h).wait_send() for h in range(2)] and None)
    assert sum(s for _, s in spots.values()) <= send_sems.shape[0]


def per_device(values, gating, out_weight, residue, decay_rate, skip_gain, cotangent):
    tokens, width = values.shape
    ctx = lax.axis_size("ctx")
    outer = ctx // INNER
    modes = decay_rate.shape[1]
    lanes = width // ctx
    rows = out_weight.shape[0]
    span = tokens * INNER
    quarter = (INNER, outer, tokens, lanes)
    chans = (outer, INNER, tokens, lanes)
    state = (outer, modes, lanes)
    slots = (outer, rows, width)
    scratch = [
        ((outer, 1, modes), F32), ((outer, modes, 128), F32), (state, F32),
        (quarter, BF16), (quarter, BF16), (chans, BF16), (chans, BF16),
        ((INNER, tokens, width), BF16), (slots, BF16), ((outer, B, lanes), F32),
        ((outer, span, lanes), F32), ((outer, span // B, modes, lanes), F32),
        ((outer, span, lanes), F32), ((span, outer * lanes), BF16), ((span, lanes), F32), ((B + 8, lanes), F32),
        (state, BF16), (state, BF16), ((outer,) + state, BF16), ((outer,) + state, BF16),
        (quarter, BF16), (quarter, BF16),
        ((INNER, tokens, width), F32), ((3, tokens, width), BF16), ((3, tokens, width), BF16),
        (slots, F32), ((outer + 1, rows, width), BF16), (slots, BF16),
    ]
    sems = pltpu.SemaphoreType.DMA((20 + 11 * outer,))
    table = residue.T if lanes % 128 == 0 else residue
    args = (values, gating, out_weight, cotangent, table, decay_rate, skip_gain.reshape(ctx, lanes))
    out = jax.ShapeDtypeStruct((tokens, width), BF16)
    macs = 3 * span * outer * lanes * width
    results = pl.pallas_call(
        functools.partial(kernel, outer),
        out_shape=[out, out, out, jax.ShapeDtypeStruct((rows, width), F32)],
        in_specs=[pl.BlockSpec(memory_space=pltpu.VMEM)] * len(args),
        out_specs=[pl.BlockSpec(memory_space=pltpu.VMEM)] * 4,
        scratch_shapes=[pltpu.VMEM(s, d) for s, d in scratch] + [sems, sems],
        compiler_params=pltpu.CompilerParams(
            collective_id=0, has_side_effects=True, vmem_limit_bytes=61 * 2**20
        ),
        cost_estimate=pl.CostEstimate(
            flops=2 * macs, bytes_accessed=6 * 2**20, transcendentals=0
        ),
    )(*args)
    steps = 2
    blocks = [
        pl.BlockSpec((r.shape[0] // steps, r.shape[1]), lambda i: (i, 0)) for r in results
    ]
    return pl.pallas_call(
        hand_over,
        grid=(steps,),
        out_shape=[jax.ShapeDtypeStruct(r.shape, r.dtype) for r in results],
        in_specs=blocks,
        out_specs=blocks,
        compiler_params=pltpu.CompilerParams(vmem_limit_bytes=58 * 2**20),
    )(*results)


def hand_over(*refs):
    for i in range(4):
        refs[4 + i][...] = refs[i][...]


def solution(mesh):
    rows = P(("parts", "ctx"), None)
    return jax.shard_map(
        per_device,
        mesh=mesh,
        in_specs=(rows, rows, rows, P("parts", None), P("parts", None), P("parts"), rows),
        out_specs=(rows,) * 4,
        check_vma=False,
    )
```
